256 devices in a mesh: row: 64 (over z, y, x_hi), col: 2 (over core), layer: 2 (over x_lo).
Axes of the slice: x: 4 (x_hi: 2, x_lo: 2; x = x_hi * 2 + x_lo), y: 4, z: 8, core: 2. Of those that a mesh axis runs over, the one named last changes fastest.
Arguments:
- a_blocks: bfloat16 [64, 128, 64, 64], P('row', ('col', 'layer')), may hold values from -6 to 6
- a_index: int32 [64, 128, 2], P('row', ('col', 'layer')), may hold values from 0 to 511, as said below
- a_count: int32 [64, 4], P('row', ('col', 'layer')), may hold values from 1 to 32, as said below
- b_blocks: bfloat16 [512, 2, 64, 64], P(('row', 'layer'), 'col'), may hold values from -0.75 to 0.75
- b_index: int32 [512, 2, 2], P(('row', 'layer'), 'col'), may hold values from 0 to 15, as said below
- b_count: int32 [128, 2], P(('row', 'layer'), 'col'), may hold values from 1 to 4, as said below
Outputs:
- product: bfloat16 [32768, 1024], P(('row', 'layer'), 'col')
The draws below stay inside these ranges and needn't reach their ends.
Inputs may be any that keep to these rules, and one draw needn't show every extreme that they name: `a_index`: within one piece the live slots name distinct (block row, inner block) positions; entry 0 is below 8, entry 1 below 512. `b_index`: within one piece the live slots name distinct (inner block, block column) positions; entry 0 is below 16, entry 1 below 8. `a_count`: some piece is full. `b_count`: some piece is full.
All inputs are finite; a program needn't handle non-finite values.
Results may differ from the reference program's by a relative error of at most 0.001.
Values may be sent and summed in bfloat16 or wider, within the bound.
No kernel may reach another device: no remote copies, remote signals or barrier semaphores. Data moves between devices by JAX's collectives and lax.ppermute only.
A program may use at most 128 MiB of HBM per device.

```python
import jax
import jax.numpy as jnp
from jax import lax

BLK = 64
NB = 2048
RW = 8
KW = 8
KPA = 512
KPB = 16
PIECE_A = 32
PIECE_B = 4
A_SLOTS = 128
B_SLOTS = 512
N_ROW = 64
N_COL = 2
N_LAYER = 2


def pick_cells(key, pieces, cells, taken):
    keys = jax.random.split(key, pieces)
    return jax.vmap(lambda single: jax.random.permutation(single, cells)[:taken])(keys).astype(jnp.int32)


def fill_counts(key, rows_n, cols_n, most):
    first, second = jax.random.split(key)
    counts = jax.random.randint(first, (rows_n * cols_n,), 1, most + 1, dtype=jnp.int32)
    where_full = jax.random.randint(second, (), 0, rows_n * cols_n, dtype=jnp.int32)
    counts = jnp.where(jnp.arange(rows_n * cols_n, dtype=jnp.int32) == where_full, most, counts)
    return counts.reshape(rows_n, cols_n).astype(jnp.int32)


def draw_a_index(key, part):
    key = jax.random.fold_in(key, 11)
    cells = pick_cells(key, N_ROW * N_COL * N_LAYER, RW * KPA, PIECE_A).reshape(N_ROW, N_COL * N_LAYER * PIECE_A)
    return jnp.stack([cells // KPA, cells % KPA], axis=-1).astype(jnp.int32)


def draw_b_index(key, part):
    key = jax.random.fold_in(key, 23)
    cells = pick_cells(key, N_ROW * N_LAYER * N_COL, KPB * KW, PIECE_B).reshape(N_ROW * N_LAYER, N_COL, PIECE_B)
    cells = jnp.transpose(cells, (0, 2, 1)).reshape(N_ROW * N_LAYER * PIECE_B, N_COL)
    return jnp.stack([cells // KW, cells % KW], axis=-1).astype(jnp.int32)


def draw_a_count(key, part):
    key = jax.random.fold_in(key, 37)
    return fill_counts(key, N_ROW, N_COL * N_LAYER, PIECE_A)


def draw_b_count(key, part):
    key = jax.random.fold_in(key, 41)
    return fill_counts(key, N_ROW * N_LAYER, N_COL, PIECE_B)


def shard_levels(stream_key, shape, cuts, smallest, top_value):
    def one(position, parts):
        draws = jax.random.uniform(jax.random.fold_in(jax.random.fold_in(stream_key, 6), position), (parts,), jnp.float32, smallest / len(cuts), top_value / len(cuts))
        return jnp.repeat(jnp.exp(draws), shape[position] // parts).reshape((-1,) + (1,) * (len(shape) - position - 1))

    level = one(*cuts[0])
    for cut in cuts[1:]:
        level = level * one(*cut)
    return level


def scatter_about(own_key, shape, deviation, reach, cuts=(), held_as=jnp.bfloat16):
    array = deviation * jax.random.normal(own_key, shape, jnp.float32)
    if cuts:
        array = array * shard_levels(own_key, shape, cuts, -0.22, 0.18)
    return jnp.clip(array, -reach, reach).astype(held_as)


def setup_inputs(seed: int = 0) -> dict:
    key_of = jax.random.split(jax.random.key(seed), 7)
    a_blocks = scatter_about(key_of[0], (N_ROW, A_SLOTS, BLK, BLK), 1.0, 6.0, ((0, 64), (1, 4)))
    a_index = draw_a_index(jax.random.fold_in(key_of[6], 71), 0)
    a_count = draw_a_count(jax.random.fold_in(key_of[6], 71), 0)
    b_blocks = scatter_about(key_of[3], (B_SLOTS, N_COL, BLK, BLK), BLK ** -0.5, 0.75, ((0, 128), (1, 2)))
    b_index = draw_b_index(jax.random.fold_in(key_of[6], 71), 0)
    b_count = draw_b_count(jax.random.fold_in(key_of[6], 71), 0)
    return dict(a_blocks=a_blocks, a_index=a_index, a_count=a_count, b_blocks=b_blocks, b_index=b_index, b_count=b_count)


def tile_product(a_vals, a_rows, a_keys, b_vals, b_keys, b_cols, row_count, col_count):
    count = b_vals.shape[0]
    hit = (a_keys[:, None, None] == b_keys[None, None, :]) & (b_cols[None, None, :] == jnp.arange(col_count, dtype=jnp.int32)[None, :, None])
    chosen = jnp.sum(jnp.where(hit, jnp.arange(count, dtype=jnp.int32)[None, None, :], 0), axis=2).astype(jnp.int32)
    found = jnp.any(hit, axis=2)
    picked = b_vals[chosen] * found[:, :, None, None].astype(b_vals.dtype)
    terms = jnp.einsum("axy,ajyz->axjz", a_vals.astype(jnp.float32), picked.astype(jnp.float32))
    place = (a_rows[:, None] == jnp.arange(row_count, dtype=jnp.int32)[None, :]).astype(jnp.float32)
    summed = jnp.dot(place.T, terms.reshape(terms.shape[0], -1), precision=lax.Precision.HIGHEST)
    return summed.reshape(row_count * BLK, col_count * BLK)


def reference(a_blocks, a_index, a_count, b_blocks, b_index, b_count):
    span = NB // N_LAYER
    slot_ids = jnp.arange(A_SLOTS, dtype=jnp.int32)
    piece_a = slot_ids // PIECE_A
    slot_bs = jnp.arange(B_SLOTS, dtype=jnp.int32)
    piece_b = slot_bs // PIECE_B

    def one_tile(flat):
        rowg = flat // N_COL
        colg = flat % N_COL
        a_vals = a_blocks[rowg]
        a_idx = a_index[rowg]
        a_live = (slot_ids % PIECE_A) < a_count[rowg][piece_a]
        a_keys = jnp.where(a_live, (piece_a % N_LAYER) * span + (piece_a // N_LAYER) * KPA + a_idx[:, 1], -1).astype(jnp.int32)
        b_vals = b_blocks[:, colg]
        b_idx = b_index[:, colg]
        b_live = (slot_bs % PIECE_B) < b_count[:, colg][piece_b]
        b_keys = jnp.where(b_live, (piece_b % N_LAYER) * span + (piece_b // N_LAYER) * KPB + b_idx[:, 0], -2).astype(jnp.int32)
        return tile_product(a_vals, a_idx[:, 0], a_keys, b_vals, b_keys, b_idx[:, 1], RW, KW).astype(jnp.bfloat16)

    tiles = lax.map(one_tile, jnp.arange(N_ROW * N_COL, dtype=jnp.int32))
    tiles = tiles.reshape(N_ROW, N_COL, RW * BLK, KW * BLK)
    return jnp.transpose(tiles, (0, 2, 1, 3)).reshape(N_ROW * RW * BLK, N_COL * KW * BLK)
```

```python
import functools

import jax
import jax.numpy as jnp
from jax import lax
from jax.experimental import pallas as pl
from jax.experimental.pallas import tpu as pltpu
from jax.sharding import PartitionSpec as P

BLK = 64
SLOTS_A = 32
SLOTS_B = 4
INNER_A = 512
INNER_B = 16
RW = 8
KW = 8
LANES = 128
TAIL = 16
RING = 8
PLANE = 8
PIECE_ROWS = SLOTS_B * BLK * BLK // LANES
STAGE_ROWS = RING * PIECE_ROWS + TAIL
HALF_ROWS = RW * BLK // 2
COLS = KW * BLK
DEAD = 255.0

Z_GROUPS = [[z * PLANE + q for z in range(RING)] for q in range(PLANE)]
PLANE_GROUPS = [[z * PLANE + q for q in range(PLANE)] for z in range(RING)]

VMEM = pl.BlockSpec(memory_space=pltpu.VMEM)
SMEM = pl.BlockSpec(memory_space=pltpu.SMEM)
ANY = pl.BlockSpec(memory_space=pl.ANY)


def pack_kernel(b_ref, index_ref, count_ref, out_ref, piece):
    z = lax.axis_index("row") // PLANE
    blocks = [b_ref[s, 0].astype(jnp.float32) for s in range(SLOTS_B)]
    for pair in range(SLOTS_B // 2):
        both = jnp.concatenate([blocks[2 * pair], blocks[2 * pair + 1]], axis=1)
        piece[pair * BLK : (pair + 1) * BLK, :] = both.astype(jnp.bfloat16)
    row = lax.broadcasted_iota(jnp.int32, (TAIL, LANES), 0)
    lane = lax.broadcasted_iota(jnp.int32, (TAIL, LANES), 1)
    codes = jnp.zeros((TAIL, LANES), jnp.float32)
    for s in range(SLOTS_B):
        code = index_ref[s, 0, 0] * KW + index_ref[s, 0, 1]
        code = jnp.where(s < count_ref[0, 0], code.astype(jnp.float32), DEAD)
        codes = jnp.where((row == 0) & (lane == z * SLOTS_B + s), code, codes)
    piece[PIECE_ROWS:, :] = codes.astype(jnp.bfloat16)
    for peer in range(RING):
        out_ref[peer] = piece[...]


def stage_kernel(ring_ref, out_ref, message, sems):
    codes = jnp.zeros((TAIL, LANES), jnp.float32)
    for z in range(RING):
        message[z * PIECE_ROWS : (z + 1) * PIECE_ROWS, :] = ring_ref[z, :PIECE_ROWS, :]
        codes = codes + ring_ref[z, PIECE_ROWS:, :].astype(jnp.float32)
    message[RING * PIECE_ROWS :, :] = codes.astype(jnp.bfloat16)
    copies = [pltpu.make_async_copy(message, out_ref.at[q], sems.at[q]) for q in range(PLANE)]
    for copy in copies:
        copy.start()
    for copy in copies:
        copy.wait()


def product_kernel(
    own_half, a_ref, index_ref, count_ref, ao_ref, oindex_ref, ocount_ref, b_ref, out_ref, codes_v, codes_s, sem
):
    col = lax.axis_index("col")
    layer = lax.axis_index("layer")
    half = layer if own_half else 1 - layer
    for q in range(PLANE):
        tail = b_ref[q, RING * PIECE_ROWS :, :].astype(jnp.float32)
        codes_v[q : q + 1, :] = tail[0:1].astype(jnp.int32)
    copy = pltpu.make_async_copy(codes_v, codes_s, sem)
    copy.start()
    out_ref[...] = jnp.zeros_like(out_ref)
    copy.wait()
    lane = lax.broadcasted_iota(jnp.int32, (BLK, LANES), 1)

    for blocks, index, count, base in (
        (a_ref, index_ref, count_ref, col * INNER_A),
        (ao_ref, oindex_ref, ocount_ref, (1 - col) * INNER_A),
    ):

        def slot(i, carry, blocks=blocks, index=index, base=base):
            row = index[0, i, 0]
            inner = base + index[0, i, 1]
            piece = inner // INNER_B
            z, q = piece // PLANE, piece % PLANE
            within = inner % INNER_B
            codes = [codes_s[q, z * SLOTS_B + s] for s in range(SLOTS_B)]
            hits = [code // KW == within for code in codes]
            mine = row // (RW // 2) == half

            @pl.when(mine & (hits[0] | hits[1] | hits[2] | hits[3]))
            def _():
                start = pl.multiple_of(z * PIECE_ROWS, PIECE_ROWS)
                at = pl.multiple_of((row % (RW // 2)) * BLK, BLK)
                a = blocks[0, i]
                for pair in range(SLOTS_B // 2):

                    @pl.when(hits[2 * pair] | hits[2 * pair + 1])
                    def _(pair=pair):
                        b = b_ref[q, pl.ds(start + pair * BLK, BLK), :]
                        terms = jnp.dot(a, b, preferred_element_type=jnp.float32)
                        for side in range(2):
                            s = 2 * pair + side

                            @pl.when(hits[s])
                            def _(s=s, side=side):
                                column = codes[s] % KW
                                right = column % 2
                                moved = jnp.where(right == side, terms, pltpu.roll(terms, BLK, 1))
                                kept = jnp.where(lane // BLK == right, moved, 0.0)
                                to = pl.multiple_of((column // 2) * LANES, LANES)
                                out_ref[pl.ds(at, BLK), pl.ds(to, LANES)] += kept

            return carry

        lax.fori_loop(0, count[0, 0], slot, 0)


def product_call(own_half, *operands):
    return pl.pallas_call(
        functools.partial(product_kernel, own_half),
        out_shape=jax.ShapeDtypeStruct((HALF_ROWS, COLS), jnp.float32),
        in_specs=[VMEM, SMEM, SMEM, VMEM, SMEM, SMEM, VMEM],
        out_specs=VMEM,
        scratch_shapes=[
            pltpu.VMEM((PLANE, LANES), jnp.int32),
            pltpu.SMEM((PLANE, LANES), jnp.int32),
            pltpu.SemaphoreType.DMA,
        ],
        cost_estimate=pl.CostEstimate(flops=100_000_000, bytes_accessed=4_000_000, transcendentals=0),
        compiler_params=pltpu.CompilerParams(vmem_limit_bytes=24 * 1024 * 1024),
        name="own_half" if own_half else "other_half",
    )(*operands)


def finish_kernel(own_ref, got_ref, out_ref):
    out_ref[...] = (own_ref[...] + got_ref[...]).astype(out_ref.dtype)


def on_device(a_blocks, a_index, a_count, b_blocks, b_index, b_count):
    swap = [(0, 1), (1, 0)]
    a_other = lax.ppermute(a_blocks, "col", swap)
    index_other = lax.ppermute(a_index, "col", swap)
    count_other = lax.ppermute(a_count, "col", swap)

    to_ring = pl.pallas_call(
        pack_kernel,
        out_shape=jax.ShapeDtypeStruct((RING, PIECE_ROWS + TAIL, LANES), jnp.bfloat16),
        in_specs=[VMEM, SMEM, SMEM],
        out_specs=VMEM,
        scratch_shapes=[pltpu.VMEM((PIECE_ROWS + TAIL, LANES), jnp.bfloat16)],
        name="pack",
    )(b_blocks, b_index, b_count)
    from_ring = lax.all_to_all(to_ring, "row", 0, 0, axis_index_groups=Z_GROUPS)
    to_plane = pl.pallas_call(
        stage_kernel,
        out_shape=jax.ShapeDtypeStruct((PLANE, STAGE_ROWS, LANES), jnp.bfloat16),
        in_specs=[VMEM],
        out_specs=ANY,
        scratch_shapes=[
            pltpu.VMEM((STAGE_ROWS, LANES), jnp.bfloat16),
            pltpu.SemaphoreType.DMA((PLANE,)),
        ],
        name="stage",
    )(from_ring)
    b_all = lax.all_to_all(to_plane, "row", 0, 0, axis_index_groups=PLANE_GROUPS)

    operands = (a_blocks, a_index, a_count, a_other, index_other, count_other, b_all)
    sent = product_call(False, *operands)
    got = lax.ppermute(sent, "layer", swap)
    own = product_call(True, *operands)
    return pl.pallas_call(
        finish_kernel,
        out_shape=jax.ShapeDtypeStruct((HALF_ROWS, COLS), jnp.bfloat16),
        in_specs=[VMEM, VMEM],
        out_specs=VMEM,
        name="finish",
    )(own, got)


def solution(mesh):
    in_specs = (
        P("row", ("col", "layer"), None, None),
        P("row", ("col", "layer"), None),
        P("row", ("col", "layer")),
        P(("row", "layer"), "col", None, None),
        P(("row", "layer"), "col", None),
        P(("row", "layer"), "col"),
    )
    out_specs = P(("row", "layer"), "col")
    return jax.shard_map(
        on_device, mesh=mesh, in_specs=in_specs, out_specs=out_specs, check_vma=False
    )
```

```python
import functools

import jax
import jax.numpy as jnp
from jax import lax
from jax.experimental import pallas as pl
from jax.experimental.pallas import tpu as pltpu
from jax.sharding import Mesh, PartitionSpec as P

BLK = 64
SLOTS_A = 32
SLOTS_B = 4
INNER_A = 512
INNER_B = 16
RW = 8
KW = 8
DEPTH = 8
SIDE = 4
PAIR = 2
RING = DEPTH * PAIR
LAYERS = 2
PEERS = SIDE * LAYERS
LANES = 128
SUB = 8
TAIL = 2 * SUB
ROWS = BLK * BLK // LANES
PIECE = SLOTS_B * ROWS
HALF = RW // LAYERS
INNER = RING * SIDE * INNER_B
SLOTS = RING * SLOTS_B
CAP = 8
NONE = RING * INNER_B
OVER = 2 * KW
STEP = 4
LIST = LANES * SLOTS_B + STEP

VMEM = pl.BlockSpec(memory_space=pltpu.VMEM)
SMEM = pl.BlockSpec(memory_space=pltpu.SMEM)
ANY = pl.BlockSpec(memory_space=pl.ANY)
LIMIT = pltpu.CompilerParams(vmem_limit_bytes=24 * 1024 * 1024)


def iota(shape, axis):
    return lax.broadcasted_iota(jnp.int32, shape, axis)


def fold_block(block):
    block = block.astype(jnp.float32)
    return jnp.concatenate([block[:ROWS], block[ROWS:]], axis=1).astype(jnp.bfloat16)


def pack_kernel(b_ref, index_ref, count_ref, aindex_ref, acount_ref, out_ref, keys_ref, piece, wide):
    at = lax.axis_index("z") * PAIR + lax.axis_index("pair")
    col = lax.axis_index("col")
    row = iota((TAIL, LANES), 0)
    codes = jnp.where(row < SUB, float(NONE), 0.0)
    for s in range(SLOTS_B):
        piece[s * ROWS : (s + 1) * ROWS, :] = fold_block(b_ref[s, 0])
        place = (at * INNER_B + index_ref[0, 0, s]).astype(jnp.float32)
        live = s < count_ref[0, 0]
        codes = jnp.where((row == s) & live, place, codes)
        codes = jnp.where((row == SUB + s) & live, index_ref[0, 1, s].astype(jnp.float32), codes)
    piece[PIECE:, :] = codes.astype(jnp.bfloat16)
    for peer in range(RING):
        out_ref[peer] = piece[...]
    wide[...] = jnp.zeros_like(wide)
    wide[0:2, 0:SLOTS_A] = aindex_ref[0]
    keys = wide[0:1, :] * INNER + col * INNER_A + wide[1:2, :]
    keys = jnp.where(iota((1, LANES), 1) < acount_ref[0, 0], keys, -1)
    keys = jnp.broadcast_to(keys, (SUB, LANES))
    keys_ref[...] = jnp.where(col == 0, keys, pltpu.roll(keys, SLOTS_A, 1))


def join_kernel(own_ref, core_ref, out_ref):
    out_ref[...] = jnp.maximum(own_ref[...], core_ref[...])


def pack_a_kernel(a_ref, keys_ref, out_ref):
    for i in range(SLOTS_A):
        out_ref[i * ROWS : (i + 1) * ROWS, :] = fold_block(a_ref[0, i])
    keys = keys_ref[...] + 1
    digits = jnp.concatenate([keys >> 6, keys & 63], axis=0)
    out_ref[SLOTS_A * ROWS :, :] = digits.astype(jnp.float32).astype(jnp.bfloat16)


def unite_kernel(own_ref, core_ref, lay_ref, diag_ref, keys_ref, out_ref, all_keys_ref):
    col = lax.axis_index("col")
    layer = lax.axis_index("layer")
    for blocks, source, side in (
        (own_ref, layer, col),
        (core_ref, layer, 1 - col),
        (lay_ref, 1 - layer, col),
        (diag_ref, 1 - layer, 1 - col),
    ):
        at = (source * 2 + side) * SLOTS_A

        def unfold(i, carry, blocks=blocks, at=at):
            start = pl.multiple_of(i * ROWS, ROWS)
            upper = blocks[pl.ds(start, ROWS), :].astype(jnp.float32)
            both = jnp.concatenate([upper, pltpu.roll(upper, BLK, 1)], axis=0)
            out_ref[at + i] = both[:, :BLK].astype(jnp.bfloat16)
            return carry

        lax.fori_loop(0, SLOTS_A, unfold, 0, unroll=4)
    own = keys_ref[...]
    other = jnp.zeros((SUB, LANES), jnp.int32)
    for blocks in (lay_ref, diag_ref):
        digits = blocks[SLOTS_A * ROWS :, :].astype(jnp.float32).astype(jnp.int32)
        other = other + digits[:SUB] * BLK + digits[SUB:]
    other = other - 1
    first = jnp.where(layer == 0, own, other)
    second = jnp.where(layer == 0, other, own)
    keys = jnp.where(iota((SUB, LANES), 1) < BLK, first, pltpu.roll(second, BLK, 1))
    all_keys_ref[...] = jnp.where(keys >> 12 == layer, keys, -1)


def select_kernel(
    ring_ref, keys0_ref, keys1_ref, keys2_ref, keys3_ref, out_ref, codes, info_v, info_s, cnt, sem
):
    y = lax.axis_index("y")
    lane = iota((SUB, LANES), 1)
    sub = iota((SUB, LANES), 0)
    left = lane < BLK
    half = jnp.where(left, 0, 1)
    wanted, weight = [], []
    for back, keys_ref in enumerate((keys0_ref, keys1_ref, keys2_ref, keys3_ref)):
        keys = keys_ref[...]
        keys = jnp.where(left, keys, pltpu.roll(keys, BLK, 1))
        mine = (keys >= 0) & (keys >> 12 == half)
        wanted.append(jnp.where(mine, keys & (INNER - 1), -1))
        low = 1 << (3 * LAYERS * ((y + SIDE - back) & (SIDE - 1)))
        weight.append(jnp.where(left, low, low << 3))
    rows = [jnp.zeros((SUB, LANES), jnp.int32) for _ in range(3)]
    for g in range(RING):
        tail = ring_ref[g, PIECE:, :].astype(jnp.float32).astype(jnp.int32)
        place, column = tail[:SUB], tail[SUB:]
        inner = ((g >> 1 << 3) + y * PAIR + (g & 1)) * INNER_B + (place & (INNER_B - 1))
        inner = jnp.where(place < NONE, inner, -2)
        counts = jnp.zeros((SUB, LANES), jnp.int32)
        for k in range(SIDE):
            counts = counts + jnp.where(inner == wanted[k], weight[k], 0)
        total = jnp.sum(counts.astype(jnp.float32), axis=1, keepdims=True).astype(jnp.int32)
        spot = (lane == g * SLOTS_B + sub) & (sub < SLOTS_B)
        for k, value in enumerate((total, place, column)):
            rows[k] = rows[k] + jnp.where(spot, value, 0)
    for k in range(3):
        info_v[k : k + 1, :] = jnp.sum(rows[k], axis=0, keepdims=True)
    copy = pltpu.make_async_copy(info_v, info_s, sem)
    copy.start()
    none = jnp.where(iota((TAIL, LANES), 0) < SUB, float(NONE), 0.0)
    for d in range(PEERS):
        codes[d] = none
    for d in range(PEERS + 1):
        cnt[d] = 0
    copy.wait()

    def some(g, carry):
        wants = [info_s[0, g * SLOTS_B + s] for s in range(SLOTS_B)]

        @pl.when((wants[0] | wants[1] | wants[2] | wants[3]) != 0)
        def _():
            for s in range(SLOTS_B):

                @pl.when(wants[s] != 0)
                def _(s=s):
                    place = jnp.full((1, LANES), info_s[1, g * SLOTS_B + s].astype(jnp.float32), jnp.float32)
                    column = jnp.full((1, LANES), info_s[2, g * SLOTS_B + s].astype(jnp.float32), jnp.float32)
                    block = ring_ref[g, s * ROWS : (s + 1) * ROWS, :]
                    for d in range(PEERS):

                        @pl.when(((wants[s] >> (3 * d)) & 7) != 0)
                        def _(d=d):
                            p = cnt[d]
                            cnt[d] = p + 1

                            @pl.when(p < CAP)
                            def _():
                                out_ref[d, pl.ds(pl.multiple_of(p * ROWS, ROWS), ROWS), :] = block
                                codes[d, pl.ds(p, 1), :] = place
                                codes[d, pl.ds(SUB + p, 1), :] = column

                            @pl.when(p >= CAP)
                            def _():
                                cnt[PEERS] = 1

        return carry

    lax.fori_loop(0, RING, some, 0)
    over = jnp.where(iota((TAIL, LANES), 0) < SUB, 0, cnt[PEERS] * OVER).astype(jnp.float32)
    for d in range(PEERS):
        out_ref[d, CAP * ROWS :, :] = (codes[d] + over).astype(jnp.bfloat16)


def all_kernel(ring_ref, out_ref, message, sems):
    first = (iota((TAIL, LANES), 0) & (SUB - 1)) < SLOTS_B
    for g in range(RING):
        message[g * PIECE : (g + 1) * PIECE, :] = ring_ref[g, :PIECE, :]
    for chunk in range(SLOTS // SUB):
        tails = [ring_ref[2 * chunk + k, PIECE:, :].astype(jnp.float32) for k in range(2)]
        tail = jnp.where(first, tails[0], pltpu.roll(tails[1], SLOTS_B, 0))
        at = RING * PIECE + chunk * TAIL
        message[at : at + TAIL, :] = tail.astype(jnp.bfloat16)
    copies = [pltpu.make_async_copy(message, out_ref.at[d], sems.at[d]) for d in range(PEERS)]
    for copy in copies:
        copy.start()
    for copy in copies:
        copy.wait()


def product_kernel(slots, chunks, a_ref, keys_ref, b_ref, out_ref, acc, info_v, info_s, todo, sem):
    lane = iota((SUB, LANES), 1)
    sub = iota((SUB, LANES), 0)
    keys = keys_ref[...]
    inner = jnp.where(keys >= 0, (keys & (INNER - 1)) + (lane >> 6) * INNER, -1)
    some = jnp.zeros((SUB, LANES), jnp.int32)
    for chunk in range(chunks):
        words = jnp.zeros((SUB, LANES), jnp.int32)
        for y in range(SIDE):
            for source in range(LAYERS):
                at = slots * ROWS + chunk * TAIL
                tail = b_ref[y * LAYERS + source, at : at + TAIL, :].astype(jnp.float32).astype(jnp.int32)
                place, column = tail[:SUB], tail[SUB:] & (KW - 1)
                piece = ((place >> 5) << 3) + y * PAIR + ((place >> 4) & 1)
                found = piece * INNER_B + (place & (INNER_B - 1)) + source * INNER
                found = jnp.where(place < NONE, found, -2)
                word = (1 << (3 * SUB + sub)) | (column << (3 * sub))
                words = words + jnp.where(found == inner, word, 0)
        some = some | words
        info_v[chunk + 2 : chunk + 3, :] = jnp.sum(words, axis=0, keepdims=True)
    some = jnp.max(jnp.where(some != 0, 1, 0), axis=0, keepdims=True)
    wide_lane = iota((LANES, LANES), 1)
    wide_sub = iota((LANES, LANES), 0)
    spread_out = jnp.where((wide_lane == wide_sub) & (some != 0), 1.0, 0.0)
    column_of = jnp.sum(spread_out, axis=1, keepdims=True)
    after = jnp.where((column_of > 0.0) & (wide_sub >= wide_lane), wide_sub, LANES)
    info_v[0:1, :] = jnp.min(after, axis=0, keepdims=True)
    info_v[1:2, :] = keys[0:1]
    copy = pltpu.make_async_copy(info_v, info_s, sem)
    copy.start()
    acc[...] = jnp.zeros_like(acc)
    copy.wait()

    def gather(state):
        i, n = state
        key = info_s[1, i]
        sender = ((key >> 5) & (SIDE - 1)) * LAYERS + (i >> 6)

        def match(p, n):
            word = info_s[2 + (p >> 3), i]
            hit = (word >> (3 * SUB + (p & 7))) & 1

            @pl.when(hit != 0)
            def _():
                todo[0, n] = i
                todo[1, n] = sender
                todo[2, n] = p
                todo[3, n] = (word >> (3 * (p & 7))) & (KW - 1)
                todo[4, n] = (key >> 10) & (HALF - 1)

            return n + hit

        n = lax.fori_loop(0, slots, match, n)
        following = jnp.where(i + 1 < LANES, info_s[0, jnp.minimum(i + 1, LANES - 1)], LANES)
        return following, n

    _, n = lax.while_loop(lambda state: state[0] < LANES, gather, (info_s[0, 0], 0))
    for k in range(STEP - 1):
        todo[0, n + k] = 0
        todo[1, n + k] = 0
        todo[2, n + k] = 0
        todo[3, n + k] = 0
        todo[4, n + k] = HALF
    side_of = iota((BLK, LANES), 1) >> 6
    left = iota((ROWS, LANES), 1) < BLK

    def several(step, carry):
        for k in range(STEP):
            at = step * STEP + k
            a = a_ref[todo[0, at]]
            start = pl.multiple_of(todo[2, at] * ROWS, ROWS)
            folded = b_ref[todo[1, at], pl.ds(start, ROWS), :].astype(jnp.float32)
            b = jnp.concatenate([jnp.where(left, folded, 0.0), jnp.where(left, 0.0, folded)], axis=0)
            terms = jnp.dot(a, b.astype(jnp.bfloat16), preferred_element_type=jnp.float32)
            terms = terms + pltpu.roll(terms, BLK, 1)
            column = todo[3, at]
            kept = jnp.where(side_of == (column & 1), terms, 0.0)
            row = pl.multiple_of(todo[4, at] * BLK, BLK)
            to = pl.multiple_of((column >> 1) * LANES, LANES)
            acc[pl.ds(row, BLK), pl.ds(to, LANES)] += kept
        return carry

    lax.fori_loop(0, (n + STEP - 1) // STEP, several, 0)
    out_ref[...] = acc[: HALF * BLK, :].astype(out_ref.dtype)


def product_call(slots, chunks, *operands):
    info = -(-(chunks + 2) // SUB) * SUB
    return pl.pallas_call(
        functools.partial(product_kernel, slots, chunks),
        out_shape=jax.ShapeDtypeStruct((HALF * BLK, KW * BLK), jnp.bfloat16),
        in_specs=[VMEM] * 3,
        out_specs=VMEM,
        scratch_shapes=[
            pltpu.VMEM((HALF * BLK + BLK, KW * BLK), jnp.float32),
            pltpu.VMEM((info, LANES), jnp.int32),
            pltpu.SMEM((info, LANES), jnp.int32),
            pltpu.SMEM((5, LIST), jnp.int32),
            pltpu.SemaphoreType.DMA,
        ],
        compiler_params=LIMIT,
        name=f"product_{slots}",
    )(*operands)


def on_device(a_blocks, a_index, a_count, b_blocks, b_index, b_count):
    swap = [(0, 1), (1, 0)]
    a_index = jnp.transpose(a_index, (0, 2, 1))
    b_index = jnp.transpose(b_index, (1, 2, 0))
    to_ring, keys = pl.pallas_call(
        pack_kernel,
        out_shape=(
            jax.ShapeDtypeStruct((RING, PIECE + TAIL, LANES), jnp.bfloat16),
            jax.ShapeDtypeStruct((SUB, LANES), jnp.int32),
        ),
        in_specs=[VMEM, SMEM, SMEM, VMEM, SMEM],
        out_specs=(VMEM, VMEM),
        scratch_shapes=[
            pltpu.VMEM((PIECE + TAIL, LANES), jnp.bfloat16),
            pltpu.VMEM((SUB, LANES), jnp.int32),
        ],
        name="pack",
    )(b_blocks, b_index, b_count, a_index, a_count)
    keys_core = lax.ppermute(keys, "col", swap)
    ring = lax.all_to_all(to_ring, ("z", "pair"), 0, 0)

    joined = pl.pallas_call(
        join_kernel,
        out_shape=jax.ShapeDtypeStruct((SUB, LANES), jnp.int32),
        in_specs=[VMEM] * 2,
        out_specs=VMEM,
        name="join_keys",
    )(keys, keys_core)
    behind = [lax.ppermute(joined, "y", [(y, (y + k) % SIDE) for y in range(SIDE)]) for k in range(1, SIDE)]
    a_blocks, _ = lax.optimization_barrier((a_blocks, joined))
    a_own = pl.pallas_call(
        pack_a_kernel,
        out_shape=jax.ShapeDtypeStruct((SLOTS_A * ROWS + TAIL, LANES), jnp.bfloat16),
        in_specs=[VMEM, VMEM],
        out_specs=VMEM,
        name="pack_a",
    )(a_blocks, keys)
    a_core = lax.ppermute(a_own, "col", swap)
    a_layer = lax.ppermute(a_own, "layer", swap)

    to_peers = pl.pallas_call(
        select_kernel,
        out_shape=jax.ShapeDtypeStruct((PEERS, CAP * ROWS + TAIL, LANES), jnp.bfloat16),
        in_specs=[VMEM] * 5,
        out_specs=VMEM,
        scratch_shapes=[
            pltpu.VMEM((PEERS, TAIL, LANES), jnp.float32),
            pltpu.VMEM((SUB, LANES), jnp.int32),
            pltpu.SMEM((SUB, LANES), jnp.int32),
            pltpu.SMEM((PEERS + 1,), jnp.int32),
            pltpu.SemaphoreType.DMA,
        ],
        name="select",
    )(ring, joined, *behind)
    received = lax.all_to_all(to_peers, ("y", "layer"), 0, 0)

    a_diag = lax.ppermute(a_layer, "col", swap)
    a_all, keys_all = pl.pallas_call(
        unite_kernel,
        out_shape=(
            jax.ShapeDtypeStruct((LANES, BLK, BLK), jnp.bfloat16),
            jax.ShapeDtypeStruct((SUB, LANES), jnp.int32),
        ),
        in_specs=[VMEM] * 5,
        out_specs=(VMEM, VMEM),
        compiler_params=LIMIT,
        name="unite_a",
    )(a_own, a_core, a_layer, a_diag, joined)

    over = jnp.max(received[:, CAP * ROWS + TAIL - 1, 0]) >= OVER

    def chosen(ring, received, a_all, keys_all):
        return product_call(CAP, 1, a_all, keys_all, received)

    def whole(ring, received, a_all, keys_all):
        rows = SLOTS * ROWS + SLOTS // SUB * TAIL
        to_all = pl.pallas_call(
            all_kernel,
            out_shape=jax.ShapeDtypeStruct((PEERS, rows, LANES), jnp.bfloat16),
            in_specs=[VMEM],
            out_specs=ANY,
            scratch_shapes=[
                pltpu.VMEM((rows, LANES), jnp.bfloat16),
                pltpu.SemaphoreType.DMA((PEERS,)),
            ],
            compiler_params=LIMIT,
            name="all_blocks",
        )(ring)
        everything = lax.all_to_all(to_all, ("y", "layer"), 0, 0)
        return product_call(SLOTS, SLOTS // SUB, a_all, keys_all, everything)

    return lax.cond(over, whole, chosen, ring, received, a_all, keys_all)


def solution(mesh):
    fine = Mesh(mesh.devices.reshape(DEPTH, SIDE, PAIR, 2, LAYERS), ("z", "y", "pair", "col", "layer"))
    row = ("z", "y", "pair")
    in_specs = (
        P(row, ("col", "layer"), None, None),
        P(row, ("col", "layer"), None),
        P(row, ("col", "layer")),
        P((*row, "layer"), "col", None, None),
        P((*row, "layer"), "col", None),
        P((*row, "layer"), "col"),
    )
    out_specs = P((*row, "layer"), "col")
    return jax.shard_map(
        on_device, mesh=fine, in_specs=in_specs, out_specs=out_specs, check_vma=False
    )
```

```python
import functools

import jax
import jax.numpy as jnp
from jax import lax
from jax.experimental import pallas as pl
from jax.experimental.pallas import tpu as pltpu
from jax.sharding import Mesh, PartitionSpec as P

BLK = 64
SLOTS_A = 32
SLOTS_B = 4
INNER_A = 512
INNER_B = 16
RW = 8
KW = 8
DEPTH = 8
SIDE = 4
PAIR = 2
RING = DEPTH * PAIR
LAYERS = 2
PEERS = SIDE * LAYERS
LANES = 128
SUB = 8
TAIL = 2 * SUB
ROWS = BLK * BLK // LANES
PIECE = SLOTS_B * ROWS
HALF = RW // LAYERS
INNER = RING * SIDE * INNER_B
SLOTS = RING * SLOTS_B
CAP = 8
NONE = RING * INNER_B
OVER = 2 * KW
STEP = 4
LIST = LANES * SLOTS_B + STEP

VMEM = pl.BlockSpec(memory_space=pltpu.VMEM)
SMEM = pl.BlockSpec(memory_space=pltpu.SMEM)
ANY = pl.BlockSpec(memory_space=pl.ANY)
LIMIT = pltpu.CompilerParams(vmem_limit_bytes=24 * 1024 * 1024)
SMALL = pltpu.CompilerParams(vmem_limit_bytes=8 * 1024 * 1024)


def iota(shape, axis):
    return lax.broadcasted_iota(jnp.int32, shape, axis)


def fold_block(block):
    block = block.astype(jnp.float32)
    return jnp.concatenate([block[:ROWS], block[ROWS:]], axis=1).astype(jnp.bfloat16)


def pack_kernel(b_ref, index_ref, count_ref, out_ref, piece):
    at = lax.axis_index("z") * PAIR + lax.axis_index("pair")
    row = iota((TAIL, LANES), 0)
    live = (row & (SUB - 1)) < jnp.broadcast_to(count_ref[...], (TAIL, LANES))
    codes = jnp.where(row < SUB, float(NONE), 0.0)
    for s in range(SLOTS_B):
        piece[s * ROWS : (s + 1) * ROWS, :] = fold_block(b_ref[s, 0])
        place = jnp.broadcast_to(at * INNER_B + index_ref[0, 0:1, s : s + 1], (TAIL, LANES)).astype(jnp.float32)
        column = jnp.broadcast_to(index_ref[0, 1:2, s : s + 1], (TAIL, LANES)).astype(jnp.float32)
        codes = jnp.where((row == s) & live, place, codes)
        codes = jnp.where((row == SUB + s) & live, column, codes)
    piece[PIECE:, :] = codes.astype(jnp.bfloat16)
    for peer in range(RING):
        out_ref[peer] = piece[...]


def pack_a_kernel(a_ref, index_ref, count_ref, out_ref, keys_ref, wide):
    col = lax.axis_index("col")
    wide[...] = jnp.zeros_like(wide)
    wide[0:2, 0:SLOTS_A] = index_ref[0]
    keys = wide[0:1, :] * INNER + col * INNER_A + wide[1:2, :]
    keys = jnp.where(iota((1, LANES), 1) < count_ref[...], keys, -1)
    keys = jnp.broadcast_to(keys, (SUB, LANES))
    keys = jnp.where(col == 0, keys, pltpu.roll(keys, SLOTS_A, 1))
    keys_ref[...] = keys
    for i in range(SLOTS_A):
        out_ref[i * ROWS : (i + 1) * ROWS, :] = fold_block(a_ref[0, i])
    digits = jnp.concatenate([(keys + 1) >> 6, (keys + 1) & 63], axis=0)
    out_ref[SLOTS_A * ROWS :, :] = digits.astype(jnp.float32).astype(jnp.bfloat16)


def join_kernel(own_ref, core_ref, out_ref):
    out_ref[...] = jnp.maximum(own_ref[...], core_ref[...])


def select_kernel(
    ring_ref, keys0_ref, keys1_ref, keys2_ref, keys3_ref, out_ref, codes, info_v, info_s, cnt, sem
):
    y = lax.axis_index("y")
    lane = iota((SUB, LANES), 1)
    sub = iota((SUB, LANES), 0)
    left = lane < BLK
    half = jnp.where(left, 0, 1)
    wanted, weight = [], []
    for back, keys_ref in enumerate((keys0_ref, keys1_ref, keys2_ref, keys3_ref)):
        keys = keys_ref[...]
        keys = jnp.where(left, keys, pltpu.roll(keys, BLK, 1))
        mine = (keys >= 0) & (keys >> 12 == half)
        wanted.append(jnp.where(mine, keys & (INNER - 1), -1))
        low = 1 << (3 * LAYERS * ((y + SIDE - back) & (SIDE - 1)))
        weight.append(jnp.where(left, low, low << 3))
    rows = [jnp.zeros((SUB, LANES), jnp.int32) for _ in range(3)]
    for g in range(RING):
        tail = ring_ref[g, PIECE:, :].astype(jnp.float32).astype(jnp.int32)
        place, column = tail[:SUB], tail[SUB:]
        inner = ((g >> 1 << 3) + y * PAIR + (g & 1)) * INNER_B + (place & (INNER_B - 1))
        inner = jnp.where(place < NONE, inner, -2)
        counts = jnp.zeros((SUB, LANES), jnp.int32)
        for k in range(SIDE):
            counts = counts + jnp.where(inner == wanted[k], weight[k], 0)
        total = jnp.sum(counts.astype(jnp.float32), axis=1, keepdims=True).astype(jnp.int32)
        spot = (lane == g * SLOTS_B + sub) & (sub < SLOTS_B)
        for k, value in enumerate((total, place, column)):
            rows[k] = rows[k] + jnp.where(spot, value, 0)
    for k in range(3):
        info_v[k : k + 1, :] = jnp.sum(rows[k], axis=0, keepdims=True)
    copy = pltpu.make_async_copy(info_v, info_s, sem)
    copy.start()
    none = jnp.where(iota((TAIL, LANES), 0) < SUB, float(NONE), 0.0)
    for d in range(PEERS):
        codes[d] = none
    for d in range(PEERS + 1):
        cnt[d] = 0
    copy.wait()

    def some(g, carry):
        wants = [info_s[0, g * SLOTS_B + s] for s in range(SLOTS_B)]

        @pl.when((wants[0] | wants[1] | wants[2] | wants[3]) != 0)
        def _():
            for s in range(SLOTS_B):

                @pl.when(wants[s] != 0)
                def _(s=s):
                    place = jnp.full((1, LANES), info_s[1, g * SLOTS_B + s].astype(jnp.float32), jnp.float32)
                    column = jnp.full((1, LANES), info_s[2, g * SLOTS_B + s].astype(jnp.float32), jnp.float32)
                    block = ring_ref[g, s * ROWS : (s + 1) * ROWS, :]
                    for d in range(PEERS):

                        @pl.when(((wants[s] >> (3 * d)) & 7) != 0)
                        def _(d=d):
                            p = cnt[d]
                            cnt[d] = p + 1

                            @pl.when(p < CAP)
                            def _():
                                out_ref[d, pl.ds(pl.multiple_of(p * ROWS, ROWS), ROWS), :] = block
                                codes[d, pl.ds(p, 1), :] = place
                                codes[d, pl.ds(SUB + p, 1), :] = column

                            @pl.when(p >= CAP)
                            def _():
                                cnt[PEERS] = 1

        return carry

    lax.fori_loop(0, RING, some, 0)
    over = jnp.where(iota((TAIL, LANES), 0) < SUB, 0, cnt[PEERS] * OVER).astype(jnp.float32)
    for d in range(PEERS):
        out_ref[d, CAP * ROWS :, :] = (codes[d] + over).astype(jnp.bfloat16)


def all_kernel(ring_ref, out_ref, message, sems):
    first = (iota((TAIL, LANES), 0) & (SUB - 1)) < SLOTS_B
    for g in range(RING):
        message[g * PIECE : (g + 1) * PIECE, :] = ring_ref[g, :PIECE, :]
    for chunk in range(SLOTS // SUB):
        tails = [ring_ref[2 * chunk + k, PIECE:, :].astype(jnp.float32) for k in range(2)]
        tail = jnp.where(first, tails[0], pltpu.roll(tails[1], SLOTS_B, 0))
        at = RING * PIECE + chunk * TAIL
        message[at : at + TAIL, :] = tail.astype(jnp.bfloat16)
    copies = [pltpu.make_async_copy(message, out_ref.at[d], sems.at[d]) for d in range(PEERS)]
    for copy in copies:
        copy.start()
    for copy in copies:
        copy.wait()


def spread(folded):
    wide = folded.astype(jnp.float32)
    left = iota((ROWS, LANES), 1) < BLK
    both = jnp.concatenate([jnp.where(left, wide, 0.0), jnp.where(left, 0.0, wide)], axis=0)
    return both.astype(jnp.bfloat16)


def unite_kernel(own_ref, core_ref, lay_ref, diag_ref, keys_ref, out_ref, all_keys_ref):
    col = lax.axis_index("col")
    layer = lax.axis_index("layer")
    for blocks, source, side in (
        (own_ref, layer, col),
        (core_ref, layer, 1 - col),
        (lay_ref, 1 - layer, col),
        (diag_ref, 1 - layer, 1 - col),
    ):
        at = (source * 2 + side) * SLOTS_A

        def one(i, carry, blocks=blocks, at=at):
            start = pl.multiple_of(i * ROWS, ROWS)
            out_ref[at + i] = spread(blocks[pl.ds(start, ROWS), :])
            return carry

        lax.fori_loop(0, SLOTS_A, one, 0, unroll=8)
    own = keys_ref[...]
    other = jnp.zeros((SUB, LANES), jnp.int32)
    for blocks in (lay_ref, diag_ref):
        digits = blocks[SLOTS_A * ROWS :, :].astype(jnp.float32).astype(jnp.int32)
        other = other + digits[:SUB] * BLK + digits[SUB:]
    other = other - 1
    first = jnp.where(layer == 0, own, other)
    second = jnp.where(layer == 0, other, own)
    keys = jnp.where(iota((SUB, LANES), 1) < BLK, first, pltpu.roll(second, BLK, 1))
    all_keys_ref[...] = jnp.where(keys >> 12 == layer, keys, -1)


def product_kernel(
    slots, chunks, a_ref, keys_ref, b_ref, out_ref, over_ref, acc, result, info_v, info_s, todo, over_s, sems, over_sem
):
    lane = iota((SUB, LANES), 1)
    sub = iota((SUB, LANES), 0)
    keys = keys_ref[...]
    inner = jnp.where(keys >= 0, (keys & (INNER - 1)) + (lane >> 6) * INNER, -1)
    some = jnp.zeros((SUB, LANES), jnp.int32)
    most = jnp.zeros((SUB, LANES), jnp.int32)
    for chunk in range(chunks):
        words = jnp.zeros((SUB, LANES), jnp.int32)
        for y in range(SIDE):
            for source in range(LAYERS):
                at = slots * ROWS + chunk * TAIL
                tail = b_ref[y * LAYERS + source, at : at + TAIL, :].astype(jnp.float32).astype(jnp.int32)
                most = jnp.maximum(most, tail[SUB:])
                place, column = tail[:SUB], tail[SUB:] & (KW - 1)
                piece = ((place >> 5) << 3) + y * PAIR + ((place >> 4) & 1)
                found = piece * INNER_B + (place & (INNER_B - 1)) + source * INNER
                found = jnp.where(place < NONE, found, -2)
                word = (1 << (3 * SUB + sub)) | (column << (3 * sub))
                words = words + jnp.where(found == inner, word, 0)
        some = some | words
        info_v[chunk + 2 : chunk + 3, :] = jnp.sum(words, axis=0, keepdims=True)
    some = jnp.max(jnp.where(some != 0, 1, 0), axis=0, keepdims=True)
    wide_lane = iota((LANES, LANES), 1)
    wide_sub = iota((LANES, LANES), 0)
    spread_out = jnp.where((wide_lane == wide_sub) & (some != 0), 1.0, 0.0)
    column_of = jnp.sum(spread_out, axis=1, keepdims=True)
    after = jnp.where((column_of > 0.0) & (wide_sub >= wide_lane), wide_sub, LANES)
    info_v[0:1, :] = jnp.min(after, axis=0, keepdims=True)
    info_v[1:2, :] = keys[0:1]
    info_v[2 + chunks : 3 + chunks, :] = most[0:1]
    copy = pltpu.make_async_copy(info_v, info_s, sems.at[0])
    copy.start()
    acc[...] = jnp.zeros_like(acc)
    copy.wait()

    over_s[0] = jnp.where(info_s[2 + chunks, 0] >= OVER, 1, 0)
    over_copy = pltpu.make_async_copy(over_s, over_ref, over_sem)
    over_copy.start()

    def gather(state):
        i, n = state
        key = info_s[1, i]
        sender = ((key >> 5) & (SIDE - 1)) * LAYERS + (i >> 6)

        for chunk in range(chunks):
            word = info_s[2 + chunk, i]

            def match(state, word=word, chunk=chunk):
                left, n = state
                low = left & -left
                p = jnp.where((low & 0xAA) != 0, 1, 0)
                p = p + jnp.where((low & 0xCC) != 0, 2, 0)
                p = p + jnp.where((low & 0xF0) != 0, 4, 0)
                todo[0, n] = i
                todo[1, n] = sender
                todo[2, n] = chunk * SUB + p
                todo[3, n] = (word >> (3 * p)) & (KW - 1)
                todo[4, n] = (key >> 10) & (HALF - 1)
                return left & (left - 1), n + 1

            left = (word >> (3 * SUB)) & 0xFF
            _, n = lax.while_loop(lambda state: state[0] != 0, match, (left, n))
        following = jnp.where(i + 1 < LANES, info_s[0, jnp.minimum(i + 1, LANES - 1)], LANES)
        return following, n

    _, n = lax.while_loop(lambda state: state[0] < LANES, gather, (info_s[0, 0], 0))
    for k in range(STEP - 1):
        todo[0, n + k] = 0
        todo[1, n + k] = 0
        todo[2, n + k] = 0
        todo[3, n + k] = 0
        todo[4, n + k] = HALF
    side_of = iota((BLK, LANES), 1) >> 6

    def several(step, carry):
        entries = [[todo[f, step * STEP + k] for f in range(5)] for k in range(STEP)]
        sums = []
        for block, sender, slot, column, _ in entries:
            start = pl.multiple_of(slot * ROWS, ROWS)
            b = spread(b_ref[sender, pl.ds(start, ROWS), :])
            b = jnp.concatenate([b, b], axis=0)
            terms = jnp.dot(a_ref[block], b, preferred_element_type=jnp.float32)
            terms = terms + pltpu.roll(terms, BLK, 1)
            sums.append(jnp.where(side_of == (column & 1), terms, 0.0))
        for (_, _, _, column, row), terms in zip(entries, sums):
            row = pl.multiple_of(row * BLK, BLK)
            to = pl.multiple_of((column >> 1) * LANES, LANES)
            acc[pl.ds(row, BLK), pl.ds(to, LANES)] += terms
        return carry

    lax.fori_loop(0, (n + STEP - 1) // STEP, several, 0)
    copies = []
    for r in range(HALF):
        rows = pl.ds(r * BLK, BLK)
        result[rows, :] = acc[rows, :].astype(result.dtype)
        copies.append(pltpu.make_async_copy(result.at[rows, :], out_ref.at[rows, :], sems.at[r]))
        copies[r].start()
    over_copy.wait()
    for copy in copies:
        copy.wait()


def product_call(slots, chunks, *operands):
    info = -(-(chunks + 3) // SUB) * SUB
    return pl.pallas_call(
        functools.partial(product_kernel, slots, chunks),
        out_shape=(
            jax.ShapeDtypeStruct((HALF * BLK, KW * BLK), jnp.bfloat16),
            jax.ShapeDtypeStruct((1,), jnp.int32),
        ),
        in_specs=[VMEM] * 3,
        out_specs=(ANY, ANY),
        scratch_shapes=[
            pltpu.VMEM((HALF * BLK + BLK, KW * BLK), jnp.float32),
            pltpu.VMEM((HALF * BLK, KW * BLK), jnp.bfloat16),
            pltpu.VMEM((info, LANES), jnp.int32),
            pltpu.SMEM((info, LANES), jnp.int32),
            pltpu.SMEM((5, LIST), jnp.int32),
            pltpu.SMEM((1,), jnp.int32),
            pltpu.SemaphoreType.DMA((HALF,)),
            pltpu.SemaphoreType.DMA,
        ],
        compiler_params=LIMIT,
        name=f"product_{slots}",
    )(*operands)


def on_device(a_blocks, a_index, a_count, b_blocks, b_index, b_count):
    swap = [(0, 1), (1, 0)]
    a_index = jnp.transpose(a_index, (0, 2, 1))
    b_index = jnp.transpose(b_index, (1, 2, 0))
    to_ring = pl.pallas_call(
        pack_kernel,
        out_shape=jax.ShapeDtypeStruct((RING, PIECE + TAIL, LANES), jnp.bfloat16),
        in_specs=[VMEM] * 3,
        out_specs=VMEM,
        scratch_shapes=[pltpu.VMEM((PIECE + TAIL, LANES), jnp.bfloat16)],
        name="pack",
    )(b_blocks, b_index, b_count)
    a_blocks, a_index, a_count, to_ring = lax.optimization_barrier((a_blocks, a_index, a_count, to_ring))
    a_own, keys = pl.pallas_call(
        pack_a_kernel,
        out_shape=(
            jax.ShapeDtypeStruct((SLOTS_A * ROWS + TAIL, LANES), jnp.bfloat16),
            jax.ShapeDtypeStruct((SUB, LANES), jnp.int32),
        ),
        in_specs=[VMEM] * 3,
        out_specs=(VMEM, VMEM),
        scratch_shapes=[pltpu.VMEM((SUB, LANES), jnp.int32)],
        compiler_params=SMALL,
        name="pack_a",
    )(a_blocks, a_index, a_count)
    keys_core = lax.ppermute(keys, "col", swap)
    ring = lax.all_to_all(to_ring, ("z", "pair"), 0, 0)

    joined = pl.pallas_call(
        join_kernel,
        out_shape=jax.ShapeDtypeStruct((SUB, LANES), jnp.int32),
        in_specs=[VMEM] * 2,
        out_specs=VMEM,
        compiler_params=SMALL,
        name="join_keys",
    )(keys, keys_core)
    behind = [lax.ppermute(joined, "y", [(y, (y + k) % SIDE) for y in range(SIDE)]) for k in range(1, SIDE)]
    a_core = lax.ppermute(a_own, "col", swap)
    a_layer = lax.ppermute(a_own, "layer", swap)

    to_peers = pl.pallas_call(
        select_kernel,
        out_shape=jax.ShapeDtypeStruct((PEERS, CAP * ROWS + TAIL, LANES), jnp.bfloat16),
        in_specs=[VMEM] * 5,
        out_specs=VMEM,
        scratch_shapes=[
            pltpu.VMEM((PEERS, TAIL, LANES), jnp.float32),
            pltpu.VMEM((SUB, LANES), jnp.int32),
            pltpu.SMEM((SUB, LANES), jnp.int32),
            pltpu.SMEM((PEERS + 1,), jnp.int32),
            pltpu.SemaphoreType.DMA,
        ],
        compiler_params=SMALL,
        name="select",
    )(ring, joined, *behind)
    received = lax.all_to_all(to_peers, ("y", "layer"), 0, 0)

    a_diag = lax.ppermute(a_layer, "col", swap)
    operands = pl.pallas_call(
        unite_kernel,
        out_shape=(
            jax.ShapeDtypeStruct((LANES, BLK, LANES), jnp.bfloat16),
            jax.ShapeDtypeStruct((SUB, LANES), jnp.int32),
        ),
        in_specs=[VMEM] * 5,
        out_specs=(VMEM, VMEM),
        compiler_params=SMALL,
        name="unite_a",
    )(a_own, a_core, a_layer, a_diag, joined)
    result, over = product_call(CAP, 1, *operands, received)

    def chosen(result, ring, *operands):
        return result

    def whole(result, ring, *operands):
        rows = SLOTS * ROWS + SLOTS // SUB * TAIL
        to_all = pl.pallas_call(
            all_kernel,
            out_shape=jax.ShapeDtypeStruct((PEERS, rows, LANES), jnp.bfloat16),
            in_specs=[VMEM],
            out_specs=ANY,
            scratch_shapes=[
                pltpu.VMEM((rows, LANES), jnp.bfloat16),
                pltpu.SemaphoreType.DMA((PEERS,)),
            ],
            compiler_params=LIMIT,
            name="all_blocks",
        )(ring)
        everything = lax.all_to_all(to_all, ("y", "layer"), 0, 0)
        return product_call(SLOTS, SLOTS // SUB, *operands, everything)[0]

    return lax.cond(over[0] > 0, whole, chosen, result, ring, *operands)


def solution(mesh):
    fine = Mesh(mesh.devices.reshape(DEPTH, SIDE, PAIR, 2, LAYERS), ("z", "y", "pair", "col", "layer"))
    row = ("z", "y", "pair")
    in_specs = (
        P(row, ("col", "layer"), None, None),
        P(row, ("col", "layer"), None),
        P(row, ("col", "layer")),
        P((*row, "layer"), "col", None, None),
        P((*row, "layer"), "col", None),
        P((*row, "layer"), "col"),
    )
    out_specs = P((*row, "layer"), "col")
    return jax.shard_map(
        on_device, mesh=fine, in_specs=in_specs, out_specs=out_specs, check_vma=False
    )
```

```python
import functools

import jax
import jax.numpy as jnp
from jax import lax
from jax.experimental import pallas as pl
from jax.experimental.pallas import tpu as pltpu
from jax.sharding import Mesh, PartitionSpec as P

BLK = 64
SLOTS_A = 32
SLOTS_B = 4
INNER_A = 512
INNER_B = 16
RW = 8
KW = 8
DEPTH = 8
SIDE = 4
PAIR = 2
RING = DEPTH * PAIR
LAYERS = 2
PEERS = SIDE * LAYERS
LANES = 128
SUB = 8
TAIL = 2 * SUB
ROWS = BLK * BLK // LANES
PIECE = SLOTS_B * ROWS
HALF = RW // LAYERS
INNER = RING * SIDE * INNER_B
SLOTS = RING * SLOTS_B
CAP = 8
NONE = RING * INNER_B
OVER = 2 * KW
STEP = 4
LIST = LANES * SLOTS_B + STEP

VMEM = pl.BlockSpec(memory_space=pltpu.VMEM)
SMEM = pl.BlockSpec(memory_space=pltpu.SMEM)
ANY = pl.BlockSpec(memory_space=pl.ANY)
LIMIT = pltpu.CompilerParams(vmem_limit_bytes=24 * 1024 * 1024)
SMALL = pltpu.CompilerParams(vmem_limit_bytes=8 * 1024 * 1024)


def iota(shape, axis):
    return lax.broadcasted_iota(jnp.int32, shape, axis)


def fold_block(block):
    block = block.astype(jnp.float32)
    return jnp.concatenate([block[:ROWS], block[ROWS:]], axis=1).astype(jnp.bfloat16)


def pack_kernel(b_ref, index_ref, count_ref, out_ref, piece):
    at = lax.axis_index("z") * PAIR + lax.axis_index("pair")
    row = iota((SUB, LANES), 0)
    live = (row & (SLOTS_B - 1)) < jnp.broadcast_to(count_ref[...], (SUB, LANES))
    codes = jnp.where(row < SLOTS_B, float(NONE), 0.0)
    for s in range(SLOTS_B):
        piece[s * ROWS : (s + 1) * ROWS, :] = fold_block(b_ref[s, 0])
        place = jnp.broadcast_to(at * INNER_B + index_ref[0, 0:1, s : s + 1], (SUB, LANES)).astype(jnp.float32)
        column = jnp.broadcast_to(index_ref[0, 1:2, s : s + 1], (SUB, LANES)).astype(jnp.float32)
        codes = jnp.where((row == s) & live, place, codes)
        codes = jnp.where((row == SLOTS_B + s) & live, column, codes)
    piece[PIECE:, :] = codes.astype(jnp.bfloat16)
    for peer in range(RING):
        out_ref[peer] = piece[...]


def pack_a_kernel(a_ref, index_ref, count_ref, out_ref, keys_ref, wide):
    col = lax.axis_index("col")
    wide[...] = jnp.zeros_like(wide)
    wide[0:2, 0:SLOTS_A] = index_ref[0]
    keys = wide[0:1, :] * INNER + col * INNER_A + wide[1:2, :]
    keys = jnp.where(iota((1, LANES), 1) < count_ref[...], keys, -1)
    keys = jnp.broadcast_to(keys, (SUB, LANES))
    keys = jnp.where(col == 0, keys, pltpu.roll(keys, SLOTS_A, 1))
    keys_ref[...] = keys
    for i in range(SLOTS_A):
        out_ref[i * ROWS : (i + 1) * ROWS, :] = fold_block(a_ref[0, i])
    digits = jnp.concatenate([(keys + 1) >> 6, (keys + 1) & 63], axis=0)
    out_ref[SLOTS_A * ROWS :, :] = digits.astype(jnp.float32).astype(jnp.bfloat16)


def join_kernel(own_ref, core_ref, out_ref):
    out_ref[...] = jnp.maximum(own_ref[...], core_ref[...])


def select_kernel(
    ring_ref, keys0_ref, keys1_ref, keys2_ref, keys3_ref, out_ref, codes, info_v, info_s, cnt, sem
):
    y = lax.axis_index("y")
    lane = iota((SUB, LANES), 1)
    sub = iota((SUB, LANES), 0)
    left = lane < BLK
    half = jnp.where(left, 0, 1)
    wanted, weight = [], []
    for back, keys_ref in enumerate((keys0_ref, keys1_ref, keys2_ref, keys3_ref)):
        keys = keys_ref[...]
        keys = jnp.where(left, keys, pltpu.roll(keys, BLK, 1))
        mine = (keys >= 0) & (keys >> 12 == half)
        wanted.append(jnp.where(mine, keys & (INNER - 1), -1))
        low = 1 << (3 * LAYERS * ((y + SIDE - back) & (SIDE - 1)))
        weight.append(jnp.where(left, low, low << 3))
    rows = [jnp.zeros((SUB, LANES), jnp.int32) for _ in range(3)]
    for g in range(RING):
        place = ring_ref[g, PIECE:, :].astype(jnp.float32).astype(jnp.int32)
        column = pltpu.roll(place, SLOTS_B, 0)
        inner = ((g >> 1 << 3) + y * PAIR + (g & 1)) * INNER_B + (place & (INNER_B - 1))
        inner = jnp.where((place < NONE) & (sub < SLOTS_B), inner, -2)
        counts = jnp.zeros((SUB, LANES), jnp.int32)
        for k in range(SIDE):
            counts = counts + jnp.where(inner == wanted[k], weight[k], 0)
        total = jnp.sum(counts.astype(jnp.float32), axis=1, keepdims=True).astype(jnp.int32)
        spot = (lane == g * SLOTS_B + sub) & (sub < SLOTS_B)
        for k, value in enumerate((total, place, column)):
            rows[k] = rows[k] + jnp.where(spot, value, 0)
    for k in range(3):
        info_v[k : k + 1, :] = jnp.sum(rows[k], axis=0, keepdims=True)
    copy = pltpu.make_async_copy(info_v, info_s, sem)
    copy.start()
    none = jnp.where(iota((TAIL, LANES), 0) < SUB, float(NONE), 0.0)
    for d in range(PEERS):
        codes[d] = none
    for d in range(PEERS + 1):
        cnt[d] = 0
    copy.wait()

    def some(g, carry):
        wants = [info_s[0, g * SLOTS_B + s] for s in range(SLOTS_B)]

        @pl.when((wants[0] | wants[1] | wants[2] | wants[3]) != 0)
        def _():
            for s in range(SLOTS_B):

                @pl.when(wants[s] != 0)
                def _(s=s):
                    place = jnp.full((1, LANES), info_s[1, g * SLOTS_B + s].astype(jnp.float32), jnp.float32)
                    column = jnp.full((1, LANES), info_s[2, g * SLOTS_B + s].astype(jnp.float32), jnp.float32)
                    block = ring_ref[g, s * ROWS : (s + 1) * ROWS, :]
                    for d in range(PEERS):

                        @pl.when(((wants[s] >> (3 * d)) & 7) != 0)
                        def _(d=d):
                            p = cnt[d]
                            cnt[d] = p + 1

                            @pl.when(p < CAP)
                            def _():
                                out_ref[d, pl.ds(pl.multiple_of(p * ROWS, ROWS), ROWS), :] = block
                                codes[d, pl.ds(p, 1), :] = place
                                codes[d, pl.ds(SUB + p, 1), :] = column

                            @pl.when(p >= CAP)
                            def _():
                                cnt[PEERS] = 1

        return carry

    lax.fori_loop(0, RING, some, 0)
    over = jnp.where(iota((TAIL, LANES), 0) < SUB, 0, cnt[PEERS] * OVER).astype(jnp.float32)
    for d in range(PEERS):
        out_ref[d, CAP * ROWS :, :] = (codes[d] + over).astype(jnp.bfloat16)


def all_kernel(ring_ref, out_ref, message, sems):
    first = iota((SUB, LANES), 0) < SLOTS_B
    for g in range(RING):
        message[g * PIECE : (g + 1) * PIECE, :] = ring_ref[g, :PIECE, :]
    for chunk in range(SLOTS // SUB):
        tails = [ring_ref[2 * chunk + k, PIECE:, :].astype(jnp.float32) for k in range(2)]
        places = jnp.where(first, tails[0], pltpu.roll(tails[1], SLOTS_B, 0))
        columns = jnp.where(first, pltpu.roll(tails[0], SLOTS_B, 0), tails[1])
        at = RING * PIECE + chunk * TAIL
        message[at : at + TAIL, :] = jnp.concatenate([places, columns], axis=0).astype(jnp.bfloat16)
    copies = [pltpu.make_async_copy(message, out_ref.at[d], sems.at[d]) for d in range(PEERS)]
    for copy in copies:
        copy.start()
    for copy in copies:
        copy.wait()


def spread(folded):
    wide = folded.astype(jnp.float32)
    left = iota((ROWS, LANES), 1) < BLK
    both = jnp.concatenate([jnp.where(left, wide, 0.0), jnp.where(left, 0.0, wide)], axis=0)
    return both.astype(jnp.bfloat16)


def unite_kernel(own_ref, core_ref, lay_ref, diag_ref, keys_ref, out_ref, all_keys_ref):
    col = lax.axis_index("col")
    layer = lax.axis_index("layer")
    for blocks, source, side in (
        (own_ref, layer, col),
        (core_ref, layer, 1 - col),
        (lay_ref, 1 - layer, col),
        (diag_ref, 1 - layer, 1 - col),
    ):
        at = (source * 2 + side) * SLOTS_A

        def one(i, carry, blocks=blocks, at=at):
            start = pl.multiple_of(i * ROWS, ROWS)
            out_ref[at + i] = spread(blocks[pl.ds(start, ROWS), :])
            return carry

        lax.fori_loop(0, SLOTS_A, one, 0, unroll=8)
    own = keys_ref[...]
    other = jnp.zeros((SUB, LANES), jnp.int32)
    for blocks in (lay_ref, diag_ref):
        digits = blocks[SLOTS_A * ROWS :, :].astype(jnp.float32).astype(jnp.int32)
        other = other + digits[:SUB] * BLK + digits[SUB:]
    other = other - 1
    first = jnp.where(layer == 0, own, other)
    second = jnp.where(layer == 0, other, own)
    keys = jnp.where(iota((SUB, LANES), 1) < BLK, first, pltpu.roll(second, BLK, 1))
    all_keys_ref[...] = jnp.where(keys >> 12 == layer, keys, -1)


def product_kernel(
    slots, chunks, a_ref, keys_ref, b_ref, out_ref, over_ref, acc, result, info_v, info_s, todo, over_s, sems, over_sem
):
    lane = iota((SUB, LANES), 1)
    sub = iota((SUB, LANES), 0)
    keys = keys_ref[...]
    inner = jnp.where(keys >= 0, (keys & (INNER - 1)) + (lane >> 6) * INNER, -1)
    some = jnp.zeros((SUB, LANES), jnp.int32)
    most = jnp.zeros((SUB, LANES), jnp.int32)
    for chunk in range(chunks):
        words = jnp.zeros((SUB, LANES), jnp.int32)
        for y in range(SIDE):
            for source in range(LAYERS):
                at = slots * ROWS + chunk * TAIL
                tail = b_ref[y * LAYERS + source, at : at + TAIL, :].astype(jnp.float32).astype(jnp.int32)
                most = jnp.maximum(most, tail[SUB:])
                place, column = tail[:SUB], tail[SUB:] & (KW - 1)
                piece = ((place >> 5) << 3) + y * PAIR + ((place >> 4) & 1)
                found = piece * INNER_B + (place & (INNER_B - 1)) + source * INNER
                found = jnp.where(place < NONE, found, -2)
                word = (1 << (3 * SUB + sub)) | (column << (3 * sub))
                words = words + jnp.where(found == inner, word, 0)
        some = some | words
        info_v[chunk + 2 : chunk + 3, :] = jnp.sum(words, axis=0, keepdims=True)
    some = jnp.max(jnp.where(some != 0, 1, 0), axis=0, keepdims=True)
    wide_lane = iota((LANES, LANES), 1)
    wide_sub = iota((LANES, LANES), 0)
    spread_out = jnp.where((wide_lane == wide_sub) & (some != 0), 1.0, 0.0)
    column_of = jnp.sum(spread_out, axis=1, keepdims=True)
    after = jnp.where((column_of > 0.0) & (wide_sub >= wide_lane), wide_sub, LANES)
    info_v[0:1, :] = jnp.min(after, axis=0, keepdims=True)
    info_v[1:2, :] = keys[0:1]
    info_v[2 + chunks : 3 + chunks, :] = most[0:1]
    copy = pltpu.make_async_copy(info_v, info_s, sems.at[0])
    copy.start()
    acc[...] = jnp.zeros_like(acc)
    copy.wait()

    over_s[0] = jnp.where(info_s[2 + chunks, 0] >= OVER, 1, 0)
    over_copy = pltpu.make_async_copy(over_s, over_ref, over_sem)
    over_copy.start()

    def gather(state):
        i, n = state
        key = info_s[1, i]
        sender = ((key >> 5) & (SIDE - 1)) * LAYERS + (i >> 6)

        for chunk in range(chunks):
            word = info_s[2 + chunk, i]

            def match(state, word=word, chunk=chunk):
                left, n = state
                low = left & -left
                p = jnp.where((low & 0xAA) != 0, 1, 0)
                p = p + jnp.where((low & 0xCC) != 0, 2, 0)
                p = p + jnp.where((low & 0xF0) != 0, 4, 0)
                todo[0, n] = i
                todo[1, n] = sender
                todo[2, n] = chunk * SUB + p
                todo[3, n] = (word >> (3 * p)) & (KW - 1)
                todo[4, n] = (key >> 10) & (HALF - 1)
                return left & (left - 1), n + 1

            left = (word >> (3 * SUB)) & 0xFF
            _, n = lax.while_loop(lambda state: state[0] != 0, match, (left, n))
        following = jnp.where(i + 1 < LANES, info_s[0, jnp.minimum(i + 1, LANES - 1)], LANES)
        return following, n

    _, n = lax.while_loop(lambda state: state[0] < LANES, gather, (info_s[0, 0], 0))
    for k in range(STEP - 1):
        todo[0, n + k] = 0
        todo[1, n + k] = 0
        todo[2, n + k] = 0
        todo[3, n + k] = 0
        todo[4, n + k] = HALF
    side_of = iota((BLK, LANES), 1) >> 6

    def several(step, carry):
        entries = [[todo[f, step * STEP + k] for f in range(5)] for k in range(STEP)]
        sums = []
        for block, sender, slot, column, _ in entries:
            start = pl.multiple_of(slot * ROWS, ROWS)
            b = spread(b_ref[sender, pl.ds(start, ROWS), :])
            b = jnp.concatenate([b, b], axis=0)
            terms = jnp.dot(a_ref[block], b, preferred_element_type=jnp.float32)
            terms = terms + pltpu.roll(terms, BLK, 1)
            sums.append(jnp.where(side_of == (column & 1), terms, 0.0))
        for (_, _, _, column, row), terms in zip(entries, sums):
            row = pl.multiple_of(row * BLK, BLK)
            to = pl.multiple_of((column >> 1) * LANES, LANES)
            acc[pl.ds(row, BLK), pl.ds(to, LANES)] += terms
        return carry

    lax.fori_loop(0, (n + STEP - 1) // STEP, several, 0)
    copies = []
    for r in range(HALF):
        rows = pl.ds(r * BLK, BLK)
        result[rows, :] = acc[rows, :].astype(result.dtype)
        copies.append(pltpu.make_async_copy(result.at[rows, :], out_ref.at[rows, :], sems.at[r]))
        copies[r].start()
    over_copy.wait()
    for copy in copies:
        copy.wait()


def product_call(slots, chunks, *operands):
    info = -(-(chunks + 3) // SUB) * SUB
    return pl.pallas_call(
        functools.partial(product_kernel, slots, chunks),
        out_shape=(
            jax.ShapeDtypeStruct((HALF * BLK, KW * BLK), jnp.bfloat16),
            jax.ShapeDtypeStruct((1,), jnp.int32),
        ),
        in_specs=[VMEM] * 3,
        out_specs=(ANY, ANY),
        scratch_shapes=[
            pltpu.VMEM((HALF * BLK + BLK, KW * BLK), jnp.float32),
            pltpu.VMEM((HALF * BLK, KW * BLK), jnp.bfloat16),
            pltpu.VMEM((info, LANES), jnp.int32),
            pltpu.SMEM((info, LANES), jnp.int32),
            pltpu.SMEM((5, LIST), jnp.int32),
            pltpu.SMEM((1,), jnp.int32),
            pltpu.SemaphoreType.DMA((HALF,)),
            pltpu.SemaphoreType.DMA,
        ],
        compiler_params=LIMIT,
        name=f"product_{slots}",
    )(*operands)


def on_device(a_blocks, a_index, a_count, b_blocks, b_index, b_count):
    swap = [(0, 1), (1, 0)]
    a_index = jnp.transpose(a_index, (0, 2, 1))
    b_index = jnp.transpose(b_index, (1, 2, 0))
    to_ring = pl.pallas_call(
        pack_kernel,
        out_shape=jax.ShapeDtypeStruct((RING, PIECE + SUB, LANES), jnp.bfloat16),
        in_specs=[VMEM] * 3,
        out_specs=VMEM,
        scratch_shapes=[pltpu.VMEM((PIECE + SUB, LANES), jnp.bfloat16)],
        name="pack",
    )(b_blocks, b_index, b_count)
    a_blocks, a_index, a_count, to_ring = lax.optimization_barrier((a_blocks, a_index, a_count, to_ring))
    a_own, keys = pl.pallas_call(
        pack_a_kernel,
        out_shape=(
            jax.ShapeDtypeStruct((SLOTS_A * ROWS + TAIL, LANES), jnp.bfloat16),
            jax.ShapeDtypeStruct((SUB, LANES), jnp.int32),
        ),
        in_specs=[VMEM] * 3,
        out_specs=(VMEM, VMEM),
        scratch_shapes=[pltpu.VMEM((SUB, LANES), jnp.int32)],
        compiler_params=SMALL,
        name="pack_a",
    )(a_blocks, a_index, a_count)
    keys_core = lax.ppermute(keys, "col", swap)
    ring = lax.all_to_all(to_ring, ("z", "pair"), 0, 0)

    joined = pl.pallas_call(
        join_kernel,
        out_shape=jax.ShapeDtypeStruct((SUB, LANES), jnp.int32),
        in_specs=[VMEM] * 2,
        out_specs=VMEM,
        compiler_params=SMALL,
        name="join_keys",
    )(keys, keys_core)
    behind = [lax.ppermute(joined, "y", [(y, (y + k) % SIDE) for y in range(SIDE)]) for k in range(1, SIDE)]
    a_core = lax.ppermute(a_own, "col", swap)
    a_layer = lax.ppermute(a_own, "layer", swap)

    to_peers = pl.pallas_call(
        select_kernel,
        out_shape=jax.ShapeDtypeStruct((PEERS, CAP * ROWS + TAIL, LANES), jnp.bfloat16),
        in_specs=[VMEM] * 5,
        out_specs=VMEM,
        scratch_shapes=[
            pltpu.VMEM((PEERS, TAIL, LANES), jnp.float32),
            pltpu.VMEM((SUB, LANES), jnp.int32),
            pltpu.SMEM((SUB, LANES), jnp.int32),
            pltpu.SMEM((PEERS + 1,), jnp.int32),
            pltpu.SemaphoreType.DMA,
        ],
        compiler_params=SMALL,
        name="select",
    )(ring, joined, *behind)
    received = lax.all_to_all(to_peers, ("y", "layer"), 0, 0)

    a_diag = lax.ppermute(a_layer, "col", swap)
    operands = pl.pallas_call(
        unite_kernel,
        out_shape=(
            jax.ShapeDtypeStruct((LANES, BLK, LANES), jnp.bfloat16),
            jax.ShapeDtypeStruct((SUB, LANES), jnp.int32),
        ),
        in_specs=[VMEM] * 5,
        out_specs=(VMEM, VMEM),
        compiler_params=SMALL,
        name="unite_a",
    )(a_own, a_core, a_layer, a_diag, joined)
    result, over = product_call(CAP, 1, *operands, received)

    def chosen(result, ring, *operands):
        return result

    def whole(result, ring, *operands):
        rows = SLOTS * ROWS + SLOTS // SUB * TAIL
        to_all = pl.pallas_call(
            all_kernel,
            out_shape=jax.ShapeDtypeStruct((PEERS, rows, LANES), jnp.bfloat16),
            in_specs=[VMEM],
            out_specs=ANY,
            scratch_shapes=[
                pltpu.VMEM((rows, LANES), jnp.bfloat16),
                pltpu.SemaphoreType.DMA((PEERS,)),
            ],
            compiler_params=LIMIT,
            name="all_blocks",
        )(ring)
        everything = lax.all_to_all(to_all, ("y", "layer"), 0, 0)
        return product_call(SLOTS, SLOTS // SUB, *operands, everything)[0]

    return lax.cond(over[0] > 0, whole, chosen, result, ring, *operands)


def solution(mesh):
    fine = Mesh(mesh.devices.reshape(DEPTH, SIDE, PAIR, 2, LAYERS), ("z", "y", "pair", "col", "layer"))
    row = ("z", "y", "pair")
    in_specs = (
        P(row, ("col", "layer"), None, None),
        P(row, ("col", "layer"), None),
        P(row, ("col", "layer")),
        P((*row, "layer"), "col", None, None),
        P((*row, "layer"), "col", None),
        P((*row, "layer"), "col"),
    )
    out_specs = P((*row, "layer"), "col")
    return jax.shard_map(
        on_device, mesh=fine, in_specs=in_specs, out_specs=out_specs, check_vma=False
    )
```

```python
import functools

import jax
import jax.numpy as jnp
from jax import lax
from jax.experimental import pallas as pl
from jax.experimental.pallas import tpu as pltpu
from jax.sharding import Mesh, PartitionSpec as P

BLK = 64
SLOTS_A = 32
SLOTS_B = 4
INNER_A = 512
INNER_B = 16
RW = 8
KW = 8
DEPTH = 8
SIDE = 4
PAIR = 2
RING = DEPTH * PAIR
LAYERS = 2
PEERS = SIDE * LAYERS
LANES = 128
SUB = 8
TAIL = 2 * SUB
ROWS = BLK * BLK // LANES
PIECE = SLOTS_B * ROWS
HALF = RW // LAYERS
INNER = RING * SIDE * INNER_B
SLOTS = RING * SLOTS_B
CAP = 8
NONE = RING * INNER_B
OVER = 2 * KW
STEP = 8
LIST = LANES * SLOTS_B + STEP

VMEM = pl.BlockSpec(memory_space=pltpu.VMEM)
SMEM = pl.BlockSpec(memory_space=pltpu.SMEM)
ANY = pl.BlockSpec(memory_space=pl.ANY)
LIMIT = pltpu.CompilerParams(vmem_limit_bytes=24 * 1024 * 1024)
SMALL = pltpu.CompilerParams(vmem_limit_bytes=8 * 1024 * 1024)


def iota(shape, axis):
    return lax.broadcasted_iota(jnp.int32, shape, axis)


def fold_block(block):
    block = block.astype(jnp.float32)
    return jnp.concatenate([block[:ROWS], block[ROWS:]], axis=1).astype(jnp.bfloat16)


def pack_kernel(b_ref, index_ref, count_ref, out_ref, piece):
    at = lax.axis_index("z") * PAIR + lax.axis_index("pair")
    row = iota((SUB, LANES), 0)
    live = (row & (SLOTS_B - 1)) < jnp.broadcast_to(count_ref[...], (SUB, LANES))
    codes = jnp.where(row < SLOTS_B, float(NONE), 0.0)
    for s in range(SLOTS_B):
        piece[s * ROWS : (s + 1) * ROWS, :] = fold_block(b_ref[s, 0])
        place = jnp.broadcast_to(at * INNER_B + index_ref[0, 0:1, s : s + 1], (SUB, LANES)).astype(jnp.float32)
        column = jnp.broadcast_to(index_ref[0, 1:2, s : s + 1], (SUB, LANES)).astype(jnp.float32)
        codes = jnp.where((row == s) & live, place, codes)
        codes = jnp.where((row == SLOTS_B + s) & live, column, codes)
    piece[PIECE:, :] = codes.astype(jnp.bfloat16)
    for peer in range(RING):
        out_ref[peer] = piece[...]


def pack_a_kernel(a_ref, index_ref, count_ref, out_ref, keys_ref, wide):
    col = lax.axis_index("col")
    wide[...] = jnp.zeros_like(wide)
    wide[0:2, 0:SLOTS_A] = index_ref[0]
    keys = wide[0:1, :] * INNER + col * INNER_A + wide[1:2, :]
    keys = jnp.where(iota((1, LANES), 1) < count_ref[...], keys, -1)
    keys = jnp.broadcast_to(keys, (SUB, LANES))
    keys = jnp.where(col == 0, keys, pltpu.roll(keys, SLOTS_A, 1))
    keys_ref[...] = keys
    for i in range(SLOTS_A):
        out_ref[i * ROWS : (i + 1) * ROWS, :] = fold_block(a_ref[0, i])
    digits = jnp.concatenate([(keys + 1) >> 6, (keys + 1) & 63], axis=0)
    out_ref[SLOTS_A * ROWS :, :] = digits.astype(jnp.float32).astype(jnp.bfloat16)


def join_kernel(own_ref, core_ref, out_ref):
    out_ref[...] = jnp.maximum(own_ref[...], core_ref[...])


def select_kernel(
    ring_ref, keys0_ref, keys1_ref, keys2_ref, keys3_ref, out_ref, codes, info_v, info_s, cnt, sem
):
    y = lax.axis_index("y")
    lane = iota((SUB, LANES), 1)
    sub = iota((SUB, LANES), 0)
    left = lane < BLK
    half = jnp.where(left, 0, 1)
    wanted, weight = [], []
    for back, keys_ref in enumerate((keys0_ref, keys1_ref, keys2_ref, keys3_ref)):
        keys = keys_ref[...]
        keys = jnp.where(left, keys, pltpu.roll(keys, BLK, 1))
        mine = (keys >= 0) & (keys >> 12 == half)
        wanted.append(jnp.where(mine, keys & (INNER - 1), -1))
        low = 1 << (3 * LAYERS * ((y + SIDE - back) & (SIDE - 1)))
        weight.append(jnp.where(left, low, low << 3))
    rows = [jnp.zeros((SUB, LANES), jnp.int32) for _ in range(3)]
    for g in range(RING):
        place = ring_ref[g, PIECE:, :].astype(jnp.float32).astype(jnp.int32)
        column = pltpu.roll(place, SLOTS_B, 0)
        inner = ((g >> 1 << 3) + y * PAIR + (g & 1)) * INNER_B + (place & (INNER_B - 1))
        inner = jnp.where((place < NONE) & (sub < SLOTS_B), inner, -2)
        counts = jnp.zeros((SUB, LANES), jnp.int32)
        for k in range(SIDE):
            counts = counts + jnp.where(inner == wanted[k], weight[k], 0)
        total = jnp.sum(counts.astype(jnp.float32), axis=1, keepdims=True).astype(jnp.int32)
        spot = (lane == g * SLOTS_B + sub) & (sub < SLOTS_B)
        for k, value in enumerate((total, place, column)):
            rows[k] = rows[k] + jnp.where(spot, value, 0)
    for k in range(3):
        info_v[k : k + 1, :] = jnp.sum(rows[k], axis=0, keepdims=True)
    copy = pltpu.make_async_copy(info_v, info_s, sem)
    copy.start()
    none = jnp.where(iota((TAIL, LANES), 0) < SUB, float(NONE), 0.0)
    for d in range(PEERS):
        codes[d] = none
    for d in range(PEERS + 1):
        cnt[d] = 0
    copy.wait()

    def some(g, carry):
        wants = [info_s[0, g * SLOTS_B + s] for s in range(SLOTS_B)]

        @pl.when((wants[0] | wants[1] | wants[2] | wants[3]) != 0)
        def _():
            for s in range(SLOTS_B):

                @pl.when(wants[s] != 0)
                def _(s=s):
                    place = jnp.full((1, LANES), info_s[1, g * SLOTS_B + s].astype(jnp.float32), jnp.float32)
                    column = jnp.full((1, LANES), info_s[2, g * SLOTS_B + s].astype(jnp.float32), jnp.float32)
                    block = ring_ref[g, s * ROWS : (s + 1) * ROWS, :]
                    for d in range(PEERS):

                        @pl.when(((wants[s] >> (3 * d)) & 7) != 0)
                        def _(d=d):
                            p = cnt[d]
                            cnt[d] = p + 1

                            @pl.when(p < CAP)
                            def _():
                                out_ref[d, pl.ds(pl.multiple_of(p * ROWS, ROWS), ROWS), :] = block
                                codes[d, pl.ds(p, 1), :] = place
                                codes[d, pl.ds(SUB + p, 1), :] = column

                            @pl.when(p >= CAP)
                            def _():
                                cnt[PEERS] = 1

        return carry

    lax.fori_loop(0, RING, some, 0)
    over = jnp.where(iota((TAIL, LANES), 0) < SUB, 0, cnt[PEERS] * OVER).astype(jnp.float32)
    for d in range(PEERS):
        out_ref[d, CAP * ROWS :, :] = (codes[d] + over).astype(jnp.bfloat16)


def all_kernel(ring_ref, out_ref, message, sems):
    first = iota((SUB, LANES), 0) < SLOTS_B
    for g in range(RING):
        message[g * PIECE : (g + 1) * PIECE, :] = ring_ref[g, :PIECE, :]
    for chunk in range(SLOTS // SUB):
        tails = [ring_ref[2 * chunk + k, PIECE:, :].astype(jnp.float32) for k in range(2)]
        places = jnp.where(first, tails[0], pltpu.roll(tails[1], SLOTS_B, 0))
        columns = jnp.where(first, pltpu.roll(tails[0], SLOTS_B, 0), tails[1])
        at = RING * PIECE + chunk * TAIL
        message[at : at + TAIL, :] = jnp.concatenate([places, columns], axis=0).astype(jnp.bfloat16)
    copies = [pltpu.make_async_copy(message, out_ref.at[d], sems.at[d]) for d in range(PEERS)]
    for copy in copies:
        copy.start()
    for copy in copies:
        copy.wait()


def spread(folded):
    wide = folded.astype(jnp.float32)
    left = iota((ROWS, LANES), 1) < BLK
    both = jnp.concatenate([jnp.where(left, wide, 0.0), jnp.where(left, 0.0, wide)], axis=0)
    return both.astype(jnp.bfloat16)


def unite_kernel(own_ref, core_ref, lay_ref, diag_ref, keys_ref, out_ref, all_keys_ref):
    col = lax.axis_index("col")
    layer = lax.axis_index("layer")
    for blocks, source, side in (
        (own_ref, layer, col),
        (core_ref, layer, 1 - col),
        (lay_ref, 1 - layer, col),
        (diag_ref, 1 - layer, 1 - col),
    ):
        at = (source * 2 + side) * SLOTS_A

        def one(i, carry, blocks=blocks, at=at):
            start = pl.multiple_of(i * ROWS, ROWS)
            out_ref[at + i] = spread(blocks[pl.ds(start, ROWS), :])
            return carry

        lax.fori_loop(0, SLOTS_A, one, 0, unroll=8)
    own = keys_ref[...]
    other = jnp.zeros((SUB, LANES), jnp.int32)
    for blocks in (lay_ref, diag_ref):
        digits = blocks[SLOTS_A * ROWS :, :].astype(jnp.float32).astype(jnp.int32)
        other = other + digits[:SUB] * BLK + digits[SUB:]
    other = other - 1
    first = jnp.where(layer == 0, own, other)
    second = jnp.where(layer == 0, other, own)
    keys = jnp.where(iota((SUB, LANES), 1) < BLK, first, pltpu.roll(second, BLK, 1))
    all_keys_ref[...] = jnp.where(keys >> 12 == layer, keys, -1)


def product_kernel(
    slots, chunks, a_ref, keys_ref, b_ref, out_ref, over_ref, acc, result, info_v, info_s, todo, over_s, sems, over_sem
):
    lane = iota((SUB, LANES), 1)
    sub = iota((SUB, LANES), 0)
    keys = keys_ref[...]
    inner = jnp.where(keys >= 0, (keys & (INNER - 1)) + (lane >> 6) * INNER, -1)
    some = jnp.zeros((SUB, LANES), jnp.int32)
    most = jnp.zeros((SUB, LANES), jnp.int32)
    for chunk in range(chunks):
        words = jnp.zeros((SUB, LANES), jnp.int32)
        for y in range(SIDE):
            for source in range(LAYERS):
                at = slots * ROWS + chunk * TAIL
                tail = b_ref[y * LAYERS + source, at : at + TAIL, :].astype(jnp.float32).astype(jnp.int32)
                most = jnp.maximum(most, tail[SUB:])
                place, column = tail[:SUB], tail[SUB:] & (KW - 1)
                piece = ((place >> 5) << 3) + y * PAIR + ((place >> 4) & 1)
                found = piece * INNER_B + (place & (INNER_B - 1)) + source * INNER
                found = jnp.where(place < NONE, found, -2)
                word = (1 << (3 * SUB + sub)) | (column << (3 * sub))
                words = words + jnp.where(found == inner, word, 0)
        some = some | words
        info_v[chunk + 2 : chunk + 3, :] = jnp.sum(words, axis=0, keepdims=True)
    some = jnp.max(jnp.where(some != 0, 1, 0), axis=0, keepdims=True)
    wide_lane = iota((LANES, LANES), 1)
    wide_sub = iota((LANES, LANES), 0)
    spread_out = jnp.where((wide_lane == wide_sub) & (some != 0), 1.0, 0.0)
    column_of = jnp.sum(spread_out, axis=1, keepdims=True)
    after = jnp.where((column_of > 0.0) & (wide_sub >= wide_lane), wide_sub, LANES)
    info_v[0:1, :] = jnp.min(after, axis=0, keepdims=True)
    info_v[1:2, :] = keys[0:1]
    info_v[2 + chunks : 3 + chunks, :] = most[0:1]
    copy = pltpu.make_async_copy(info_v, info_s, sems.at[0])
    copy.start()
    acc[...] = jnp.zeros_like(acc)
    copy.wait()

    over_s[0] = jnp.where(info_s[2 + chunks, 0] >= OVER, 1, 0)
    over_copy = pltpu.make_async_copy(over_s, over_ref, over_sem)
    over_copy.start()

    def gather(state):
        i, n = state
        key = info_s[1, i]
        sender = ((key >> 5) & (SIDE - 1)) * LAYERS + (i >> 6)

        for chunk in range(chunks):
            word = info_s[2 + chunk, i]

            def match(state, word=word, chunk=chunk):
                left, n = state
                low = left & -left
                p = jnp.where((low & 0xAA) != 0, 1, 0)
                p = p + jnp.where((low & 0xCC) != 0, 2, 0)
                p = p + jnp.where((low & 0xF0) != 0, 4, 0)
                todo[0, n] = i
                todo[1, n] = sender
                todo[2, n] = chunk * SUB + p
                todo[3, n] = (word >> (3 * p)) & (KW - 1)
                todo[4, n] = (key >> 10) & (HALF - 1)
                return left & (left - 1), n + 1

            left = (word >> (3 * SUB)) & 0xFF
            _, n = lax.while_loop(lambda state: state[0] != 0, match, (left, n))
        following = jnp.where(i + 1 < LANES, info_s[0, jnp.minimum(i + 1, LANES - 1)], LANES)
        return following, n

    _, n = lax.while_loop(lambda state: state[0] < LANES, gather, (info_s[0, 0], 0))
    for k in range(STEP - 1):
        todo[0, n + k] = 0
        todo[1, n + k] = 0
        todo[2, n + k] = 0
        todo[3, n + k] = 0
        todo[4, n + k] = HALF
    side_of = iota((BLK, LANES), 1) >> 6

    def several(step, carry):
        entries = [[todo[f, step * STEP + k] for f in range(5)] for k in range(STEP)]
        sums = []
        for block, sender, slot, column, _ in entries:
            start = pl.multiple_of(slot * ROWS, ROWS)
            b = spread(b_ref[sender, pl.ds(start, ROWS), :])
            b = jnp.concatenate([b, b], axis=0)
            terms = jnp.dot(a_ref[block], b, preferred_element_type=jnp.float32)
            terms = terms + pltpu.roll(terms, BLK, 1)
            sums.append(jnp.where(side_of == (column & 1), terms, 0.0))
        for (_, _, _, column, row), terms in zip(entries, sums):
            row = pl.multiple_of(row * BLK, BLK)
            to = pl.multiple_of((column >> 1) * LANES, LANES)
            acc[pl.ds(row, BLK), pl.ds(to, LANES)] += terms
        return carry

    lax.fori_loop(0, (n + STEP - 1) // STEP, several, 0)
    copies = []
    for r in range(HALF):
        rows = pl.ds(r * BLK, BLK)
        result[rows, :] = acc[rows, :].astype(result.dtype)
        copies.append(pltpu.make_async_copy(result.at[rows, :], out_ref.at[rows, :], sems.at[r]))
        copies[r].start()
    over_copy.wait()
    for copy in copies:
        copy.wait()


def product_call(slots, chunks, *operands):
    info = -(-(chunks + 3) // SUB) * SUB
    return pl.pallas_call(
        functools.partial(product_kernel, slots, chunks),
        out_shape=(
            jax.ShapeDtypeStruct((HALF * BLK, KW * BLK), jnp.bfloat16),
            jax.ShapeDtypeStruct((1,), jnp.int32),
        ),
        in_specs=[VMEM] * 3,
        out_specs=(ANY, ANY),
        scratch_shapes=[
            pltpu.VMEM((HALF * BLK + BLK, KW * BLK), jnp.float32),
            pltpu.VMEM((HALF * BLK, KW * BLK), jnp.bfloat16),
            pltpu.VMEM((info, LANES), jnp.int32),
            pltpu.SMEM((info, LANES), jnp.int32),
            pltpu.SMEM((5, LIST), jnp.int32),
            pltpu.SMEM((1,), jnp.int32),
            pltpu.SemaphoreType.DMA((HALF,)),
            pltpu.SemaphoreType.DMA,
        ],
        compiler_params=LIMIT,
        name=f"product_{slots}",
    )(*operands)


def on_device(a_blocks, a_index, a_count, b_blocks, b_index, b_count):
    swap = [(0, 1), (1, 0)]
    a_index = jnp.transpose(a_index, (0, 2, 1))
    b_index = jnp.transpose(b_index, (1, 2, 0))
    to_ring = pl.pallas_call(
        pack_kernel,
        out_shape=jax.ShapeDtypeStruct((RING, PIECE + SUB, LANES), jnp.bfloat16),
        in_specs=[VMEM] * 3,
        out_specs=VMEM,
        scratch_shapes=[pltpu.VMEM((PIECE + SUB, LANES), jnp.bfloat16)],
        name="pack",
    )(b_blocks, b_index, b_count)
    a_blocks, a_index, a_count, to_ring = lax.optimization_barrier((a_blocks, a_index, a_count, to_ring))
    a_own, keys = pl.pallas_call(
        pack_a_kernel,
        out_shape=(
            jax.ShapeDtypeStruct((SLOTS_A * ROWS + TAIL, LANES), jnp.bfloat16),
            jax.ShapeDtypeStruct((SUB, LANES), jnp.int32),
        ),
        in_specs=[VMEM] * 3,
        out_specs=(VMEM, VMEM),
        scratch_shapes=[pltpu.VMEM((SUB, LANES), jnp.int32)],
        compiler_params=SMALL,
        name="pack_a",
    )(a_blocks, a_index, a_count)
    keys_core = lax.ppermute(keys, "col", swap)
    ring = lax.all_to_all(to_ring, ("z", "pair"), 0, 0)

    joined = pl.pallas_call(
        join_kernel,
        out_shape=jax.ShapeDtypeStruct((SUB, LANES), jnp.int32),
        in_specs=[VMEM] * 2,
        out_specs=VMEM,
        compiler_params=SMALL,
        name="join_keys",
    )(keys, keys_core)
    behind = [lax.ppermute(joined, "y", [(y, (y + k) % SIDE) for y in range(SIDE)]) for k in range(1, SIDE)]
    a_core = lax.ppermute(a_own, "col", swap)
    a_layer = lax.ppermute(a_own, "layer", swap)

    to_peers = pl.pallas_call(
        select_kernel,
        out_shape=jax.ShapeDtypeStruct((PEERS, CAP * ROWS + TAIL, LANES), jnp.bfloat16),
        in_specs=[VMEM] * 5,
        out_specs=VMEM,
        scratch_shapes=[
            pltpu.VMEM((PEERS, TAIL, LANES), jnp.float32),
            pltpu.VMEM((SUB, LANES), jnp.int32),
            pltpu.SMEM((SUB, LANES), jnp.int32),
            pltpu.SMEM((PEERS + 1,), jnp.int32),
            pltpu.SemaphoreType.DMA,
        ],
        compiler_params=SMALL,
        name="select",
    )(ring, joined, *behind)
    received = lax.all_to_all(to_peers, ("y", "layer"), 0, 0)

    a_diag = lax.ppermute(a_layer, "col", swap)
    operands = pl.pallas_call(
        unite_kernel,
        out_shape=(
            jax.ShapeDtypeStruct((LANES, BLK, LANES), jnp.bfloat16),
            jax.ShapeDtypeStruct((SUB, LANES), jnp.int32),
        ),
        in_specs=[VMEM] * 5,
        out_specs=(VMEM, VMEM),
        compiler_params=SMALL,
        name="unite_a",
    )(a_own, a_core, a_layer, a_diag, joined)
    result, over = product_call(CAP, 1, *operands, received)

    def chosen(result, ring, *operands):
        return result

    def whole(result, ring, *operands):
        rows = SLOTS * ROWS + SLOTS // SUB * TAIL
        to_all = pl.pallas_call(
            all_kernel,
            out_shape=jax.ShapeDtypeStruct((PEERS, rows, LANES), jnp.bfloat16),
            in_specs=[VMEM],
            out_specs=ANY,
            scratch_shapes=[
                pltpu.VMEM((rows, LANES), jnp.bfloat16),
                pltpu.SemaphoreType.DMA((PEERS,)),
            ],
            compiler_params=LIMIT,
            name="all_blocks",
        )(ring)
        everything = lax.all_to_all(to_all, ("y", "layer"), 0, 0)
        return product_call(SLOTS, SLOTS // SUB, *operands, everything)[0]

    return lax.cond(over[0] > 0, whole, chosen, result, ring, *operands)


def solution(mesh):
    fine = Mesh(mesh.devices.reshape(DEPTH, SIDE, PAIR, 2, LAYERS), ("z", "y", "pair", "col", "layer"))
    row = ("z", "y", "pair")
    in_specs = (
        P(row, ("col", "layer"), None, None),
        P(row, ("col", "layer"), None),
        P(row, ("col", "layer")),
        P((*row, "layer"), "col", None, None),
        P((*row, "layer"), "col", None),
        P((*row, "layer"), "col"),
    )
    out_specs = P((*row, "layer"), "col")
    return jax.shard_map(
        on_device, mesh=fine, in_specs=in_specs, out_specs=out_specs, check_vma=False
    )
```

```python
import functools

import jax
import jax.numpy as jnp
from jax import lax
from jax.experimental import pallas as pl
from jax.experimental.pallas import tpu as pltpu
from jax.sharding import Mesh, PartitionSpec as P

BLK = 64
SLOTS_A = 32
SLOTS_B = 4
INNER_A = 512
INNER_B = 16
RW = 8
KW = 8
DEPTH = 8
SIDE = 4
PAIR = 2
RING = DEPTH * PAIR
LAYERS = 2
PEERS = SIDE * LAYERS
LANES = 128
SUB = 8
TAIL = 2 * SUB
ROWS = BLK * BLK // LANES
PIECE = SLOTS_B * ROWS
HALF = RW // LAYERS
INNER = RING * SIDE * INNER_B
SLOTS = RING * SLOTS_B
CAP = 8
NONE = RING * INNER_B
OVER = 2 * KW
STEP = 8
LIST = LANES * SLOTS_B + STEP

VMEM = pl.BlockSpec(memory_space=pltpu.VMEM)
SMEM = pl.BlockSpec(memory_space=pltpu.SMEM)
ANY = pl.BlockSpec(memory_space=pl.ANY)
LIMIT = pltpu.CompilerParams(vmem_limit_bytes=24 * 1024 * 1024)
SMALL = pltpu.CompilerParams(vmem_limit_bytes=8 * 1024 * 1024)


def iota(shape, axis):
    return lax.broadcasted_iota(jnp.int32, shape, axis)


def fold_block(block):
    block = block.astype(jnp.float32)
    return jnp.concatenate([block[:ROWS], block[ROWS:]], axis=1).astype(jnp.bfloat16)


def pack_kernel(b_ref, index_ref, count_ref, out_ref, piece):
    at = lax.axis_index("pair") * DEPTH + lax.axis_index("z")
    row = iota((SUB, LANES), 0)
    live = (row & (SLOTS_B - 1)) < jnp.broadcast_to(count_ref[...], (SUB, LANES))
    codes = jnp.where(row < SLOTS_B, float(NONE), 0.0)
    for s in range(SLOTS_B):
        piece[s * ROWS : (s + 1) * ROWS, :] = fold_block(b_ref[s, 0])
        place = jnp.broadcast_to(at * INNER_B + index_ref[0, 0:1, s : s + 1], (SUB, LANES)).astype(jnp.float32)
        column = jnp.broadcast_to(index_ref[0, 1:2, s : s + 1], (SUB, LANES)).astype(jnp.float32)
        codes = jnp.where((row == s) & live, place, codes)
        codes = jnp.where((row == SLOTS_B + s) & live, column, codes)
    piece[PIECE:, :] = codes.astype(jnp.bfloat16)
    for peer in range(RING):
        out_ref[peer] = piece[...]


def pack_a_kernel(a_ref, index_ref, count_ref, out_ref, keys_ref, wide):
    col = lax.axis_index("col")
    wide[...] = jnp.zeros_like(wide)
    wide[0:2, 0:SLOTS_A] = index_ref[0]
    keys = wide[0:1, :] * INNER + col * INNER_A + wide[1:2, :]
    keys = jnp.where(iota((1, LANES), 1) < count_ref[...], keys, -1)
    keys = jnp.broadcast_to(keys, (SUB, LANES))
    keys = jnp.where(col == 0, keys, pltpu.roll(keys, SLOTS_A, 1))
    keys_ref[...] = keys
    for i in range(SLOTS_A):
        out_ref[i * ROWS : (i + 1) * ROWS, :] = fold_block(a_ref[0, i])
    digits = jnp.concatenate([(keys + 1) >> 6, (keys + 1) & 63], axis=0)
    out_ref[SLOTS_A * ROWS :, :] = digits.astype(jnp.float32).astype(jnp.bfloat16)


def join_kernel(own_ref, core_ref, out_ref):
    out_ref[...] = jnp.maximum(own_ref[...], core_ref[...])


def select_kernel(
    ring_ref, keys0_ref, keys1_ref, keys2_ref, keys3_ref, out_ref, codes, info_v, info_s, cnt, sem
):
    y = lax.axis_index("y")
    lane = iota((SUB, LANES), 1)
    sub = iota((SUB, LANES), 0)
    left = lane < BLK
    half = jnp.where(left, 0, 1)
    wanted, weight = [], []
    for back, keys_ref in enumerate((keys0_ref, keys1_ref, keys2_ref, keys3_ref)):
        keys = keys_ref[...]
        keys = jnp.where(left, keys, pltpu.roll(keys, BLK, 1))
        mine = (keys >= 0) & (keys >> 12 == half)
        wanted.append(jnp.where(mine, keys & (INNER - 1), -1))
        low = 1 << (3 * ((y + SIDE - back) & (SIDE - 1)))
        weight.append(jnp.where(left, low, low << (3 * SIDE)))
    rows = [jnp.zeros((SUB, LANES), jnp.int32) for _ in range(3)]
    for g in range(RING):
        place = ring_ref[g, PIECE:, :].astype(jnp.float32).astype(jnp.int32)
        column = pltpu.roll(place, SLOTS_B, 0)
        inner = ((g % DEPTH) * SIDE * PAIR + y * PAIR + g // DEPTH) * INNER_B + (place & (INNER_B - 1))
        inner = jnp.where((place < NONE) & (sub < SLOTS_B), inner, -2)
        counts = jnp.zeros((SUB, LANES), jnp.int32)
        for k in range(SIDE):
            counts = counts + jnp.where(inner == wanted[k], weight[k], 0)
        total = jnp.sum(counts.astype(jnp.float32), axis=1, keepdims=True).astype(jnp.int32)
        spot = (lane == g * SLOTS_B + sub) & (sub < SLOTS_B)
        for k, value in enumerate((total, place, column)):
            rows[k] = rows[k] + jnp.where(spot, value, 0)
    for k in range(3):
        info_v[k : k + 1, :] = jnp.sum(rows[k], axis=0, keepdims=True)
    copy = pltpu.make_async_copy(info_v, info_s, sem)
    copy.start()
    none = jnp.where(iota((TAIL, LANES), 0) < SUB, float(NONE), 0.0)
    for d in range(PEERS):
        codes[d] = none
    for d in range(PEERS + 1):
        cnt[d] = 0
    copy.wait()

    def some(g, carry):
        wants = [info_s[0, g * SLOTS_B + s] for s in range(SLOTS_B)]

        @pl.when((wants[0] | wants[1] | wants[2] | wants[3]) != 0)
        def _():
            for s in range(SLOTS_B):

                @pl.when(wants[s] != 0)
                def _(s=s):
                    place = jnp.full((1, LANES), info_s[1, g * SLOTS_B + s].astype(jnp.float32), jnp.float32)
                    column = jnp.full((1, LANES), info_s[2, g * SLOTS_B + s].astype(jnp.float32), jnp.float32)
                    block = ring_ref[g, s * ROWS : (s + 1) * ROWS, :]
                    for d in range(PEERS):

                        @pl.when(((wants[s] >> (3 * d)) & 7) != 0)
                        def _(d=d):
                            p = cnt[d]
                            cnt[d] = p + 1

                            @pl.when(p < CAP)
                            def _():
                                out_ref[d, pl.ds(pl.multiple_of(p * ROWS, ROWS), ROWS), :] = block
                                codes[d, pl.ds(p, 1), :] = place
                                codes[d, pl.ds(SUB + p, 1), :] = column

                            @pl.when(p >= CAP)
                            def _():
                                cnt[PEERS] = 1

        return carry

    lax.fori_loop(0, RING, some, 0)
    over = jnp.where(iota((TAIL, LANES), 0) < SUB, 0, cnt[PEERS] * OVER).astype(jnp.float32)
    for d in range(PEERS):
        out_ref[d, CAP * ROWS :, :] = (codes[d] + over).astype(jnp.bfloat16)


def all_kernel(ring_ref, out_ref, message, sems):
    first = iota((SUB, LANES), 0) < SLOTS_B
    for g in range(RING):
        message[g * PIECE : (g + 1) * PIECE, :] = ring_ref[g, :PIECE, :]
    for chunk in range(SLOTS // SUB):
        tails = [ring_ref[2 * chunk + k, PIECE:, :].astype(jnp.float32) for k in range(2)]
        places = jnp.where(first, tails[0], pltpu.roll(tails[1], SLOTS_B, 0))
        columns = jnp.where(first, pltpu.roll(tails[0], SLOTS_B, 0), tails[1])
        at = RING * PIECE + chunk * TAIL
        message[at : at + TAIL, :] = jnp.concatenate([places, columns], axis=0).astype(jnp.bfloat16)
    copies = [pltpu.make_async_copy(message, out_ref.at[d], sems.at[d]) for d in range(PEERS)]
    for copy in copies:
        copy.start()
    for copy in copies:
        copy.wait()


def spread(folded):
    wide = folded.astype(jnp.float32)
    left = iota((ROWS, LANES), 1) < BLK
    both = jnp.concatenate([jnp.where(left, wide, 0.0), jnp.where(left, 0.0, wide)], axis=0)
    return both.astype(jnp.bfloat16)


def unite_kernel(own_ref, core_ref, lay_ref, diag_ref, keys_ref, out_ref, all_keys_ref):
    col = lax.axis_index("col")
    layer = lax.axis_index("layer")
    for blocks, source, side in (
        (own_ref, layer, col),
        (core_ref, layer, 1 - col),
        (lay_ref, 1 - layer, col),
        (diag_ref, 1 - layer, 1 - col),
    ):
        at = (source * 2 + side) * SLOTS_A

        def one(i, carry, blocks=blocks, at=at):
            start = pl.multiple_of(i * ROWS, ROWS)
            out_ref[at + i] = spread(blocks[pl.ds(start, ROWS), :])
            return carry

        lax.fori_loop(0, SLOTS_A, one, 0, unroll=8)
    own = keys_ref[...]
    other = jnp.zeros((SUB, LANES), jnp.int32)
    for blocks in (lay_ref, diag_ref):
        digits = blocks[SLOTS_A * ROWS :, :].astype(jnp.float32).astype(jnp.int32)
        other = other + digits[:SUB] * BLK + digits[SUB:]
    other = other - 1
    first = jnp.where(layer == 0, own, other)
    second = jnp.where(layer == 0, other, own)
    keys = jnp.where(iota((SUB, LANES), 1) < BLK, first, pltpu.roll(second, BLK, 1))
    all_keys_ref[...] = jnp.where(keys >> 12 == layer, keys, -1)


def product_kernel(
    slots, chunks, a_ref, keys_ref, b_ref, out_ref, over_ref, acc, result, info_v, info_s, todo, over_s, sems, over_sem
):
    lane = iota((SUB, LANES), 1)
    sub = iota((SUB, LANES), 0)
    keys = keys_ref[...]
    inner = jnp.where(keys >= 0, (keys & (INNER - 1)) + (lane >> 6) * INNER, -1)
    some = jnp.zeros((SUB, LANES), jnp.int32)
    most = jnp.zeros((SUB, LANES), jnp.int32)
    for chunk in range(chunks):
        words = jnp.zeros((SUB, LANES), jnp.int32)
        for y in range(SIDE):
            for source in range(LAYERS):
                at = slots * ROWS + chunk * TAIL
                tail = b_ref[source * SIDE + y, at : at + TAIL, :].astype(jnp.float32).astype(jnp.int32)
                most = jnp.maximum(most, tail[SUB:])
                place, column = tail[:SUB], tail[SUB:] & (KW - 1)
                piece = (((place >> 4) & (DEPTH - 1)) << 3) + y * PAIR + (place >> 7)
                found = piece * INNER_B + (place & (INNER_B - 1)) + source * INNER
                found = jnp.where(place < NONE, found, -2)
                word = (1 << (3 * SUB + sub)) | (column << (3 * sub))
                words = words + jnp.where(found == inner, word, 0)
        some = some | words
        info_v[chunk + 2 : chunk + 3, :] = jnp.sum(words, axis=0, keepdims=True)
    some = jnp.max(jnp.where(some != 0, 1, 0), axis=0, keepdims=True)
    wide_lane = iota((LANES, LANES), 1)
    wide_sub = iota((LANES, LANES), 0)
    spread_out = jnp.where((wide_lane == wide_sub) & (some != 0), 1.0, 0.0)
    column_of = jnp.sum(spread_out, axis=1, keepdims=True)
    after = jnp.where((column_of > 0.0) & (wide_sub >= wide_lane), wide_sub, LANES)
    info_v[0:1, :] = jnp.min(after, axis=0, keepdims=True)
    info_v[1:2, :] = keys[0:1]
    info_v[2 + chunks : 3 + chunks, :] = most[0:1]
    copy = pltpu.make_async_copy(info_v, info_s, sems.at[0])
    copy.start()
    acc[...] = jnp.zeros_like(acc)
    copy.wait()

    over_s[0] = jnp.where(info_s[2 + chunks, 0] >= OVER, 1, 0)
    over_copy = pltpu.make_async_copy(over_s, over_ref, over_sem)
    over_copy.start()

    def gather(state):
        i, n = state
        key = info_s[1, i]
        sender = (i >> 6) * SIDE + ((key >> 5) & (SIDE - 1))

        for chunk in range(chunks):
            word = info_s[2 + chunk, i]

            def match(state, word=word, chunk=chunk):
                left, n = state
                low = left & -left
                p = jnp.where((low & 0xAA) != 0, 1, 0)
                p = p + jnp.where((low & 0xCC) != 0, 2, 0)
                p = p + jnp.where((low & 0xF0) != 0, 4, 0)
                todo[0, n] = i
                todo[1, n] = sender
                todo[2, n] = chunk * SUB + p
                todo[3, n] = (word >> (3 * p)) & (KW - 1)
                todo[4, n] = (key >> 10) & (HALF - 1)
                return left & (left - 1), n + 1

            left = (word >> (3 * SUB)) & 0xFF
            _, n = lax.while_loop(lambda state: state[0] != 0, match, (left, n))
        following = jnp.where(i + 1 < LANES, info_s[0, jnp.minimum(i + 1, LANES - 1)], LANES)
        return following, n

    _, n = lax.while_loop(lambda state: state[0] < LANES, gather, (info_s[0, 0], 0))
    for k in range(STEP - 1):
        todo[0, n + k] = 0
        todo[1, n + k] = 0
        todo[2, n + k] = 0
        todo[3, n + k] = 0
        todo[4, n + k] = HALF
    side_of = iota((BLK, LANES), 1) >> 6

    def several(step, carry):
        entries = [[todo[f, step * STEP + k] for f in range(5)] for k in range(STEP)]
        sums = []
        for block, sender, slot, column, _ in entries:
            start = pl.multiple_of(slot * ROWS, ROWS)
            b = spread(b_ref[sender, pl.ds(start, ROWS), :])
            b = jnp.concatenate([b, b], axis=0)
            terms = jnp.dot(a_ref[block], b, preferred_element_type=jnp.float32)
            terms = terms + pltpu.roll(terms, BLK, 1)
            sums.append(jnp.where(side_of == (column & 1), terms, 0.0))
        for (_, _, _, column, row), terms in zip(entries, sums):
            row = pl.multiple_of(row * BLK, BLK)
            to = pl.multiple_of((column >> 1) * LANES, LANES)
            acc[pl.ds(row, BLK), pl.ds(to, LANES)] += terms
        return carry

    lax.fori_loop(0, (n + STEP - 1) // STEP, several, 0)
    copies = []
    for r in range(HALF):
        rows = pl.ds(r * BLK, BLK)
        result[rows, :] = acc[rows, :].astype(result.dtype)
        copies.append(pltpu.make_async_copy(result.at[rows, :], out_ref.at[rows, :], sems.at[r]))
        copies[r].start()
    over_copy.wait()
    for copy in copies:
        copy.wait()


def product_call(slots, chunks, *operands):
    info = -(-(chunks + 3) // SUB) * SUB
    return pl.pallas_call(
        functools.partial(product_kernel, slots, chunks),
        out_shape=(
            jax.ShapeDtypeStruct((HALF * BLK, KW * BLK), jnp.bfloat16),
            jax.ShapeDtypeStruct((1,), jnp.int32),
        ),
        in_specs=[VMEM] * 3,
        out_specs=(ANY, ANY),
        scratch_shapes=[
            pltpu.VMEM((HALF * BLK + BLK, KW * BLK), jnp.float32),
            pltpu.VMEM((HALF * BLK, KW * BLK), jnp.bfloat16),
            pltpu.VMEM((info, LANES), jnp.int32),
            pltpu.SMEM((info, LANES), jnp.int32),
            pltpu.SMEM((5, LIST), jnp.int32),
            pltpu.SMEM((1,), jnp.int32),
            pltpu.SemaphoreType.DMA((HALF,)),
            pltpu.SemaphoreType.DMA,
        ],
        compiler_params=LIMIT,
        name=f"product_{slots}",
    )(*operands)


def on_device(a_blocks, a_index, a_count, b_blocks, b_index, b_count):
    swap = [(0, 1), (1, 0)]
    a_index = jnp.transpose(a_index, (0, 2, 1))
    b_index = jnp.transpose(b_index, (1, 2, 0))
    to_ring = pl.pallas_call(
        pack_kernel,
        out_shape=jax.ShapeDtypeStruct((RING, PIECE + SUB, LANES), jnp.bfloat16),
        in_specs=[VMEM] * 3,
        out_specs=VMEM,
        scratch_shapes=[pltpu.VMEM((PIECE + SUB, LANES), jnp.bfloat16)],
        name="pack",
    )(b_blocks, b_index, b_count)
    a_blocks, a_index, a_count, to_ring = lax.optimization_barrier((a_blocks, a_index, a_count, to_ring))
    a_own, keys = pl.pallas_call(
        pack_a_kernel,
        out_shape=(
            jax.ShapeDtypeStruct((SLOTS_A * ROWS + TAIL, LANES), jnp.bfloat16),
            jax.ShapeDtypeStruct((SUB, LANES), jnp.int32),
        ),
        in_specs=[VMEM] * 3,
        out_specs=(VMEM, VMEM),
        scratch_shapes=[pltpu.VMEM((SUB, LANES), jnp.int32)],
        compiler_params=SMALL,
        name="pack_a",
    )(a_blocks, a_index, a_count)
    keys_core = lax.ppermute(keys, "col", swap)
    ring = lax.all_to_all(to_ring, ("pair", "z"), 0, 0)

    joined = pl.pallas_call(
        join_kernel,
        out_shape=jax.ShapeDtypeStruct((SUB, LANES), jnp.int32),
        in_specs=[VMEM] * 2,
        out_specs=VMEM,
        compiler_params=SMALL,
        name="join_keys",
    )(keys, keys_core)
    behind = [lax.ppermute(joined, "y", [(y, (y + k) % SIDE) for y in range(SIDE)]) for k in range(1, SIDE)]
    a_core = lax.ppermute(a_own, "col", swap)
    a_layer = lax.ppermute(a_own, "layer", swap)

    to_peers = pl.pallas_call(
        select_kernel,
        out_shape=jax.ShapeDtypeStruct((PEERS, CAP * ROWS + TAIL, LANES), jnp.bfloat16),
        in_specs=[VMEM] * 5,
        out_specs=VMEM,
        scratch_shapes=[
            pltpu.VMEM((PEERS, TAIL, LANES), jnp.float32),
            pltpu.VMEM((SUB, LANES), jnp.int32),
            pltpu.SMEM((SUB, LANES), jnp.int32),
            pltpu.SMEM((PEERS + 1,), jnp.int32),
            pltpu.SemaphoreType.DMA,
        ],
        compiler_params=SMALL,
        name="select",
    )(ring, joined, *behind)
    received = lax.all_to_all(to_peers, ("layer", "y"), 0, 0)

    a_diag = lax.ppermute(a_layer, "col", swap)
    operands = pl.pallas_call(
        unite_kernel,
        out_shape=(
            jax.ShapeDtypeStruct((LANES, BLK, LANES), jnp.bfloat16),
            jax.ShapeDtypeStruct((SUB, LANES), jnp.int32),
        ),
        in_specs=[VMEM] * 5,
        out_specs=(VMEM, VMEM),
        compiler_params=SMALL,
        name="unite_a",
    )(a_own, a_core, a_layer, a_diag, joined)
    result, over = product_call(CAP, 1, *operands, received)

    def chosen(result, ring, *operands):
        return result

    def whole(result, ring, *operands):
        rows = SLOTS * ROWS + SLOTS // SUB * TAIL
        to_all = pl.pallas_call(
            all_kernel,
            out_shape=jax.ShapeDtypeStruct((PEERS, rows, LANES), jnp.bfloat16),
            in_specs=[VMEM],
            out_specs=ANY,
            scratch_shapes=[
                pltpu.VMEM((rows, LANES), jnp.bfloat16),
                pltpu.SemaphoreType.DMA((PEERS,)),
            ],
            compiler_params=LIMIT,
            name="all_blocks",
        )(ring)
        everything = lax.all_to_all(to_all, ("layer", "y"), 0, 0)
        return product_call(SLOTS, SLOTS // SUB, *operands, everything)[0]

    return lax.cond(over[0] > 0, whole, chosen, result, ring, *operands)


def solution(mesh):
    fine = Mesh(mesh.devices.reshape(DEPTH, SIDE, PAIR, 2, LAYERS), ("z", "y", "pair", "col", "layer"))
    row = ("z", "y", "pair")
    in_specs = (
        P(row, ("col", "layer"), None, None),
        P(row, ("col", "layer"), None),
        P(row, ("col", "layer")),
        P((*row, "layer"), "col", None, None),
        P((*row, "layer"), "col", None),
        P((*row, "layer"), "col"),
    )
    out_specs = P((*row, "layer"), "col")
    return jax.shard_map(
        on_device, mesh=fine, in_specs=in_specs, out_specs=out_specs, check_vma=False
    )
```

```python
import functools

import jax
import jax.numpy as jnp
from jax import lax
from jax.experimental import pallas as pl
from jax.experimental.pallas import tpu as pltpu
from jax.sharding import Mesh, PartitionSpec as P

BLK = 64
SLOTS_A = 32
SLOTS_B = 4
INNER_A = 512
INNER_B = 16
RW = 8
KW = 8
DEPTH = 8
SIDE = 4
PAIR = 2
RING = DEPTH * PAIR
LAYERS = 2
PEERS = SIDE * LAYERS
LANES = 128
SUB = 8
TAIL = 2 * SUB
ROWS = BLK * BLK // LANES
PIECE = SLOTS_B * ROWS
HALF = RW // LAYERS
INNER = RING * SIDE * INNER_B
SLOTS = RING * SLOTS_B
CAP = 8
NONE = RING * INNER_B
OVER = 2 * KW
STEP = 8
LIST = LANES * SLOTS_B + STEP

VMEM = pl.BlockSpec(memory_space=pltpu.VMEM)
SMEM = pl.BlockSpec(memory_space=pltpu.SMEM)
ANY = pl.BlockSpec(memory_space=pl.ANY)
LIMIT = pltpu.CompilerParams(vmem_limit_bytes=24 * 1024 * 1024)
SMALL = pltpu.CompilerParams(vmem_limit_bytes=8 * 1024 * 1024)


def iota(shape, axis):
    return lax.broadcasted_iota(jnp.int32, shape, axis)


def fold_block(block):
    block = block.astype(jnp.float32)
    return jnp.concatenate([block[:ROWS], block[ROWS:]], axis=1).astype(jnp.bfloat16)


def pack_kernel(b_ref, index_ref, count_ref, out_ref, piece):
    at = lax.axis_index("pair") * DEPTH + lax.axis_index("z")
    row = iota((SUB, LANES), 0)
    live = (row & (SLOTS_B - 1)) < jnp.broadcast_to(count_ref[...], (SUB, LANES))
    codes = jnp.where(row < SLOTS_B, float(NONE), 0.0)
    for s in range(SLOTS_B):
        piece[s * ROWS : (s + 1) * ROWS, :] = fold_block(b_ref[s, 0])
        place = jnp.broadcast_to(at * INNER_B + index_ref[0, 0:1, s : s + 1], (SUB, LANES)).astype(jnp.float32)
        column = jnp.broadcast_to(index_ref[0, 1:2, s : s + 1], (SUB, LANES)).astype(jnp.float32)
        codes = jnp.where((row == s) & live, place, codes)
        codes = jnp.where((row == SLOTS_B + s) & live, column, codes)
    piece[PIECE:, :] = codes.astype(jnp.bfloat16)
    for peer in range(RING):
        out_ref[peer] = piece[...]


def pack_a_kernel(a_ref, index_ref, count_ref, out_ref, keys_ref, wide):
    col = lax.axis_index("col")
    wide[...] = jnp.zeros_like(wide)
    wide[0:2, 0:SLOTS_A] = index_ref[0]
    keys = wide[0:1, :] * INNER + col * INNER_A + wide[1:2, :]
    keys = jnp.where(iota((1, LANES), 1) < count_ref[...], keys, -1)
    keys = jnp.broadcast_to(keys, (SUB, LANES))
    keys = jnp.where(col == 0, keys, pltpu.roll(keys, SLOTS_A, 1))
    keys_ref[...] = keys
    for i in range(SLOTS_A):
        out_ref[i * ROWS : (i + 1) * ROWS, :] = fold_block(a_ref[0, i])
    digits = jnp.concatenate([(keys + 1) >> 6, (keys + 1) & 63], axis=0)
    out_ref[SLOTS_A * ROWS :, :] = digits.astype(jnp.float32).astype(jnp.bfloat16)


def join_kernel(own_ref, core_ref, out_ref):
    out_ref[...] = jnp.maximum(own_ref[...], core_ref[...])


def select_kernel(
    ring_ref, keys0_ref, keys1_ref, keys2_ref, keys3_ref, out_ref, codes, info_v, info_s, cnt, sem
):
    y = lax.axis_index("y")
    lane = iota((SUB, LANES), 1)
    sub = iota((SUB, LANES), 0)
    left = lane < BLK
    half = jnp.where(left, 0, 1)
    wanted, weight = [], []
    for back, keys_ref in enumerate((keys0_ref, keys1_ref, keys2_ref, keys3_ref)):
        keys = keys_ref[...]
        keys = jnp.where(left, keys, pltpu.roll(keys, BLK, 1))
        mine = (keys >= 0) & (keys >> 12 == half)
        wanted.append(jnp.where(mine, keys & (INNER - 1), -1))
        low = 1 << (3 * ((y + SIDE - back) & (SIDE - 1)))
        weight.append(jnp.where(left, low, low << (3 * SIDE)))
    rows = [jnp.zeros((SUB, LANES), jnp.int32) for _ in range(3)]
    for g in range(RING):
        place = ring_ref[g, PIECE:, :].astype(jnp.float32).astype(jnp.int32)
        column = pltpu.roll(place, SLOTS_B, 0)
        inner = ((g % DEPTH) * SIDE * PAIR + y * PAIR + g // DEPTH) * INNER_B + (place & (INNER_B - 1))
        inner = jnp.where((place < NONE) & (sub < SLOTS_B), inner, -2)
        counts = jnp.zeros((SUB, LANES), jnp.int32)
        for k in range(SIDE):
            counts = counts + jnp.where(inner == wanted[k], weight[k], 0)
        total = jnp.sum(counts.astype(jnp.float32), axis=1, keepdims=True).astype(jnp.int32)
        spot = (lane == g * SLOTS_B + sub) & (sub < SLOTS_B)
        for k, value in enumerate((total, place, column)):
            rows[k] = rows[k] + jnp.where(spot, value, 0)
    for k in range(3):
        info_v[k : k + 1, :] = jnp.sum(rows[k], axis=0, keepdims=True)
    copy = pltpu.make_async_copy(info_v, info_s, sem)
    copy.start()
    none = jnp.where(left, float(NONE), 0.0)
    for d in range(PEERS):
        codes[d] = none
    for d in range(PEERS + 1):
        cnt[d] = 0
    copy.wait()

    def some(g, carry):
        wants = [info_s[0, g * SLOTS_B + s] for s in range(SLOTS_B)]

        @pl.when((wants[0] | wants[1] | wants[2] | wants[3]) != 0)
        def _():
            for s in range(SLOTS_B):

                @pl.when(wants[s] != 0)
                def _(s=s):
                    place = jnp.full((1, LANES), info_s[1, g * SLOTS_B + s].astype(jnp.float32), jnp.float32)
                    column = jnp.full((1, LANES), info_s[2, g * SLOTS_B + s].astype(jnp.float32), jnp.float32)
                    block = ring_ref[g, s * ROWS : (s + 1) * ROWS, :]
                    for d in range(PEERS):

                        @pl.when(((wants[s] >> (3 * d)) & 7) != 0)
                        def _(d=d):
                            p = cnt[d]
                            cnt[d] = p + 1

                            @pl.when(p < CAP)
                            def _():
                                out_ref[d, pl.ds(pl.multiple_of(p * ROWS, ROWS), ROWS), :] = block
                                codes[d, pl.ds(p, 1), :] = jnp.where(left[0:1], place, column)

                            @pl.when(p >= CAP)
                            def _():
                                cnt[PEERS] = 1

        return carry

    lax.fori_loop(0, RING, some, 0)
    over = jnp.where(left, 0, cnt[PEERS] * OVER).astype(jnp.float32)
    for d in range(PEERS):
        out_ref[d, CAP * ROWS :, :] = (codes[d] + over).astype(jnp.bfloat16)


def all_kernel(ring_ref, out_ref, message, sems):
    first = iota((SUB, LANES), 0) < SLOTS_B
    for g in range(RING):
        message[g * PIECE : (g + 1) * PIECE, :] = ring_ref[g, :PIECE, :]
    for chunk in range(SLOTS // SUB):
        tails = [ring_ref[2 * chunk + k, PIECE:, :].astype(jnp.float32) for k in range(2)]
        places = jnp.where(first, tails[0], pltpu.roll(tails[1], SLOTS_B, 0))
        columns = jnp.where(first, pltpu.roll(tails[0], SLOTS_B, 0), tails[1])
        both = jnp.where(iota((SUB, LANES), 1) < BLK, places, columns)
        at = RING * PIECE + chunk * TAIL
        message[at : at + TAIL, :] = jnp.concatenate([both, both], axis=0).astype(jnp.bfloat16)
    copies = [pltpu.make_async_copy(message, out_ref.at[d], sems.at[d]) for d in range(PEERS)]
    for copy in copies:
        copy.start()
    for copy in copies:
        copy.wait()


def spread(folded):
    wide = folded.astype(jnp.float32)
    left = iota((ROWS, LANES), 1) < BLK
    both = jnp.concatenate([jnp.where(left, wide, 0.0), jnp.where(left, 0.0, wide)], axis=0)
    return both.astype(jnp.bfloat16)


def unite_kernel(own_ref, core_ref, lay_ref, diag_ref, keys_ref, out_ref, all_keys_ref):
    col = lax.axis_index("col")
    layer = lax.axis_index("layer")
    for blocks, source, side in (
        (own_ref, layer, col),
        (core_ref, layer, 1 - col),
        (lay_ref, 1 - layer, col),
        (diag_ref, 1 - layer, 1 - col),
    ):
        at = (source * 2 + side) * SLOTS_A

        def one(i, carry, blocks=blocks, at=at):
            start = pl.multiple_of(i * ROWS, ROWS)
            out_ref[at + i] = spread(blocks[pl.ds(start, ROWS), :])
            return carry

        lax.fori_loop(0, SLOTS_A, one, 0, unroll=8)
    own = keys_ref[...]
    other = jnp.zeros((SUB, LANES), jnp.int32)
    for blocks in (lay_ref, diag_ref):
        digits = blocks[SLOTS_A * ROWS :, :].astype(jnp.float32).astype(jnp.int32)
        other = other + digits[:SUB] * BLK + digits[SUB:]
    other = other - 1
    first = jnp.where(layer == 0, own, other)
    second = jnp.where(layer == 0, other, own)
    keys = jnp.where(iota((SUB, LANES), 1) < BLK, first, pltpu.roll(second, BLK, 1))
    all_keys_ref[...] = jnp.where(keys >> 12 == layer, keys, -1)


def product_kernel(
    slots, chunks, a_ref, keys_ref, b_ref, out_ref, over_ref, acc, result, info_v, info_s, todo, over_s, sems, over_sem
):
    lane = iota((SUB, LANES), 1)
    sub = iota((SUB, LANES), 0)
    keys = keys_ref[...]
    inner = jnp.where(keys >= 0, (keys & (INNER - 1)) + (lane >> 6) * INNER, -1)
    some = jnp.zeros((SUB, LANES), jnp.int32)
    most = jnp.zeros((SUB, LANES), jnp.int32)
    for chunk in range(chunks):
        words = jnp.zeros((SUB, LANES), jnp.int32)
        for y in range(SIDE):
            for source in range(LAYERS):
                at = slots * ROWS + chunk * TAIL
                tail = b_ref[source * SIDE + y, at : at + SUB, :].astype(jnp.float32).astype(jnp.int32)
                turned = pltpu.roll(tail, BLK, 1)
                place = jnp.where(lane < BLK, tail, turned)
                column = jnp.where(lane < BLK, turned, tail)
                most = jnp.maximum(most, column)
                column = column & (KW - 1)
                piece = (((place >> 4) & (DEPTH - 1)) << 3) + y * PAIR + (place >> 7)
                found = piece * INNER_B + (place & (INNER_B - 1)) + source * INNER
                found = jnp.where(place < NONE, found, -2)
                word = (1 << (3 * SUB + sub)) | (column << (3 * sub))
                words = words + jnp.where(found == inner, word, 0)
        some = some | words
        info_v[chunk + 2 : chunk + 3, :] = jnp.sum(words, axis=0, keepdims=True)
    some = jnp.max(jnp.where(some != 0, 1, 0), axis=0, keepdims=True)
    wide_lane = iota((LANES, LANES), 1)
    wide_sub = iota((LANES, LANES), 0)
    spread_out = jnp.where((wide_lane == wide_sub) & (some != 0), 1.0, 0.0)
    column_of = jnp.sum(spread_out, axis=1, keepdims=True)
    after = jnp.where((column_of > 0.0) & (wide_sub >= wide_lane), wide_sub, LANES)
    info_v[0:1, :] = jnp.min(after, axis=0, keepdims=True)
    info_v[1:2, :] = keys[0:1]
    info_v[2 + chunks : 3 + chunks, :] = most[0:1]
    copy = pltpu.make_async_copy(info_v, info_s, sems.at[0])
    copy.start()
    acc[...] = jnp.zeros_like(acc)
    copy.wait()

    over_s[0] = jnp.where(info_s[2 + chunks, 0] >= OVER, 1, 0)
    over_copy = pltpu.make_async_copy(over_s, over_ref, over_sem)
    over_copy.start()

    def gather(state):
        i, n = state
        key = info_s[1, i]
        sender = (i >> 6) * SIDE + ((key >> 5) & (SIDE - 1))

        for chunk in range(chunks):
            word = info_s[2 + chunk, i]

            def match(state, word=word, chunk=chunk):
                left, n = state
                low = left & -left
                p = jnp.where((low & 0xAA) != 0, 1, 0)
                p = p + jnp.where((low & 0xCC) != 0, 2, 0)
                p = p + jnp.where((low & 0xF0) != 0, 4, 0)
                todo[0, n] = i
                todo[1, n] = sender
                todo[2, n] = chunk * SUB + p
                todo[3, n] = (word >> (3 * p)) & (KW - 1)
                todo[4, n] = (key >> 10) & (HALF - 1)
                return left & (left - 1), n + 1

            left = (word >> (3 * SUB)) & 0xFF
            _, n = lax.while_loop(lambda state: state[0] != 0, match, (left, n))
        following = jnp.where(i + 1 < LANES, info_s[0, jnp.minimum(i + 1, LANES - 1)], LANES)
        return following, n

    _, n = lax.while_loop(lambda state: state[0] < LANES, gather, (info_s[0, 0], 0))
    for k in range(STEP - 1):
        todo[0, n + k] = 0
        todo[1, n + k] = 0
        todo[2, n + k] = 0
        todo[3, n + k] = 0
        todo[4, n + k] = HALF
    side_of = iota((BLK, LANES), 1) >> 6

    def several(step, carry):
        entries = [[todo[f, step * STEP + k] for f in range(5)] for k in range(STEP)]
        sums = []
        for block, sender, slot, column, _ in entries:
            start = pl.multiple_of(slot * ROWS, ROWS)
            b = spread(b_ref[sender, pl.ds(start, ROWS), :])
            b = jnp.concatenate([b, b], axis=0)
            terms = jnp.dot(a_ref[block], b, preferred_element_type=jnp.float32)
            terms = terms + pltpu.roll(terms, BLK, 1)
            sums.append(jnp.where(side_of == (column & 1), terms, 0.0))
        for (_, _, _, column, row), terms in zip(entries, sums):
            row = pl.multiple_of(row * BLK, BLK)
            to = pl.multiple_of((column >> 1) * LANES, LANES)
            acc[pl.ds(row, BLK), pl.ds(to, LANES)] += terms
        return carry

    lax.fori_loop(0, (n + STEP - 1) // STEP, several, 0)
    copies = []
    for r in range(HALF):
        rows = pl.ds(r * BLK, BLK)
        result[rows, :] = acc[rows, :].astype(result.dtype)
        copies.append(pltpu.make_async_copy(result.at[rows, :], out_ref.at[rows, :], sems.at[r]))
        copies[r].start()
    over_copy.wait()
    for copy in copies:
        copy.wait()


def product_call(slots, chunks, *operands):
    info = -(-(chunks + 3) // SUB) * SUB
    return pl.pallas_call(
        functools.partial(product_kernel, slots, chunks),
        out_shape=(
            jax.ShapeDtypeStruct((HALF * BLK, KW * BLK), jnp.bfloat16),
            jax.ShapeDtypeStruct((1,), jnp.int32),
        ),
        in_specs=[VMEM] * 3,
        out_specs=(ANY, ANY),
        scratch_shapes=[
            pltpu.VMEM((HALF * BLK + BLK, KW * BLK), jnp.float32),
            pltpu.VMEM((HALF * BLK, KW * BLK), jnp.bfloat16),
            pltpu.VMEM((info, LANES), jnp.int32),
            pltpu.SMEM((info, LANES), jnp.int32),
            pltpu.SMEM((5, LIST), jnp.int32),
            pltpu.SMEM((1,), jnp.int32),
            pltpu.SemaphoreType.DMA((HALF,)),
            pltpu.SemaphoreType.DMA,
        ],
        compiler_params=LIMIT,
        name=f"product_{slots}",
    )(*operands)


def on_device(a_blocks, a_index, a_count, b_blocks, b_index, b_count):
    swap = [(0, 1), (1, 0)]
    a_index = jnp.transpose(a_index, (0, 2, 1))
    b_index = jnp.transpose(b_index, (1, 2, 0))
    to_ring = pl.pallas_call(
        pack_kernel,
        out_shape=jax.ShapeDtypeStruct((RING, PIECE + SUB, LANES), jnp.bfloat16),
        in_specs=[VMEM] * 3,
        out_specs=VMEM,
        scratch_shapes=[pltpu.VMEM((PIECE + SUB, LANES), jnp.bfloat16)],
        name="pack",
    )(b_blocks, b_index, b_count)
    a_blocks, a_index, a_count, to_ring = lax.optimization_barrier((a_blocks, a_index, a_count, to_ring))
    a_own, keys = pl.pallas_call(
        pack_a_kernel,
        out_shape=(
            jax.ShapeDtypeStruct((SLOTS_A * ROWS + TAIL, LANES), jnp.bfloat16),
            jax.ShapeDtypeStruct((SUB, LANES), jnp.int32),
        ),
        in_specs=[VMEM] * 3,
        out_specs=(VMEM, VMEM),
        scratch_shapes=[pltpu.VMEM((SUB, LANES), jnp.int32)],
        compiler_params=SMALL,
        name="pack_a",
    )(a_blocks, a_index, a_count)
    keys_core = lax.ppermute(keys, "col", swap)
    ring = lax.all_to_all(to_ring, ("pair", "z"), 0, 0)

    joined = pl.pallas_call(
        join_kernel,
        out_shape=jax.ShapeDtypeStruct((SUB, LANES), jnp.int32),
        in_specs=[VMEM] * 2,
        out_specs=VMEM,
        compiler_params=SMALL,
        name="join_keys",
    )(keys, keys_core)
    behind = [lax.ppermute(joined, "y", [(y, (y + k) % SIDE) for y in range(SIDE)]) for k in range(1, SIDE)]
    a_core = lax.ppermute(a_own, "col", swap)
    a_layer = lax.ppermute(a_own, "layer", swap)

    to_peers = pl.pallas_call(
        select_kernel,
        out_shape=jax.ShapeDtypeStruct((PEERS, CAP * ROWS + SUB, LANES), jnp.bfloat16),
        in_specs=[VMEM] * 5,
        out_specs=VMEM,
        scratch_shapes=[
            pltpu.VMEM((PEERS, SUB, LANES), jnp.float32),
            pltpu.VMEM((SUB, LANES), jnp.int32),
            pltpu.SMEM((SUB, LANES), jnp.int32),
            pltpu.SMEM((PEERS + 1,), jnp.int32),
            pltpu.SemaphoreType.DMA,
        ],
        compiler_params=SMALL,
        name="select",
    )(ring, joined, *behind)
    received = lax.all_to_all(to_peers, ("layer", "y"), 0, 0)

    a_diag = lax.ppermute(a_layer, "col", swap)
    operands = pl.pallas_call(
        unite_kernel,
        out_shape=(
            jax.ShapeDtypeStruct((LANES, BLK, LANES), jnp.bfloat16),
            jax.ShapeDtypeStruct((SUB, LANES), jnp.int32),
        ),
        in_specs=[VMEM] * 5,
        out_specs=(VMEM, VMEM),
        compiler_params=SMALL,
        name="unite_a",
    )(a_own, a_core, a_layer, a_diag, joined)
    result, over = product_call(CAP, 1, *operands, received)

    def chosen(result, ring, *operands):
        return result

    def whole(result, ring, *operands):
        rows = SLOTS * ROWS + SLOTS // SUB * TAIL
        to_all = pl.pallas_call(
            all_kernel,
            out_shape=jax.ShapeDtypeStruct((PEERS, rows, LANES), jnp.bfloat16),
            in_specs=[VMEM],
            out_specs=ANY,
            scratch_shapes=[
                pltpu.VMEM((rows, LANES), jnp.bfloat16),
                pltpu.SemaphoreType.DMA((PEERS,)),
            ],
            compiler_params=LIMIT,
            name="all_blocks",
        )(ring)
        everything = lax.all_to_all(to_all, ("layer", "y"), 0, 0)
        return product_call(SLOTS, SLOTS // SUB, *operands, everything)[0]

    return lax.cond(over[0] > 0, whole, chosen, result, ring, *operands)


def solution(mesh):
    fine = Mesh(mesh.devices.reshape(DEPTH, SIDE, PAIR, 2, LAYERS), ("z", "y", "pair", "col", "layer"))
    row = ("z", "y", "pair")
    in_specs = (
        P(row, ("col", "layer"), None, None),
        P(row, ("col", "layer"), None),
        P(row, ("col", "layer")),
        P((*row, "layer"), "col", None, None),
        P((*row, "layer"), "col", None),
        P((*row, "layer"), "col"),
    )
    out_specs = P((*row, "layer"), "col")
    return jax.shard_map(
        on_device, mesh=fine, in_specs=in_specs, out_specs=out_specs, check_vma=False
    )
```
